128 devices in a mesh: grp: 4 (over x_lo, core), blk: 32 (over y, z, x_hi).
Axes of the slice: x: 4 (x_hi: 2, x_lo: 2; x = x_hi * 2 + x_lo), y: 4, z: 4, core: 2. Of those that a mesh axis runs over, the one named last changes fastest.
Arguments:
- train_grads: bfloat16 [524288, 1024], P(('grp', 'blk'))
- targets: bfloat16 [16384, 1024], P(('grp', 'blk')), may hold values from -6 to 6
Outputs:
- scores: bfloat16 [524288, 384], P(('grp', 'blk'))
The draws below stay inside these ranges and needn't reach their ends.
All inputs are finite; a program needn't handle non-finite values.
Results may differ from the reference program's by a relative error of at most 0.014.
Values may be sent and summed in bfloat16 or wider, within the bound.
A program may use at most 128 MiB of HBM per device.

```python
import math
import jax
import jax.numpy as jnp
from jax import lax

PROJ = 1024
TR_DEV = 4096
TGT_BLK = 128
VISITS = 3
TRAIN = 524288
TARGETS = 16384
N_GRP = 4
N_BLK = 32


def draw_train_grads(key, part):
    key = jax.random.fold_in(key, 1)
    key_base, key_cols, key_rows, key_common, key_sources, key_polarity, key_ranking = jax.random.split(key, 7)
    base = jax.random.normal(key_base, (TRAIN, PROJ), jnp.float32)
    ranking = jax.random.permutation(key_ranking, PROJ).astype(jnp.float32)
    strength = (ranking + 1.0) ** (-0.75)
    harmonic = sum((float(number + 1) ** (-1.5) for number in range(PROJ)))
    level = math.sqrt(3.75 * PROJ / (8.0 * harmonic))
    sources = jax.random.randint(key_sources, (8, PROJ), 0, PROJ)
    polarity = 2.0 * jax.random.randint(key_polarity, (8, PROJ), 0, 2).astype(jnp.float32) - 1.0
    mixed = 0.5 * base
    for number in range(8):
        coupling = level * polarity[number] * strength[sources[number]]
        mixed = mixed + jnp.take(base, sources[number], axis=1) * coupling
    columns = jnp.exp(jax.random.uniform(key_cols, (PROJ,), jnp.float32, 0.0, math.log(10.0)))
    rise = jnp.exp(math.log(3.0) * jnp.arange(TRAIN, dtype=jnp.float32) / TRAIN)
    rough = jnp.exp(jax.random.uniform(key_rows, (TRAIN, 1), jnp.float32, 0.0, math.log(2.0)))
    grads = mixed * columns * rise[:, None] * rough
    return grads.astype(jnp.bfloat16)


def steps_of(key, extent, cuts, least, top_value):
    level = 1.0
    for position, parts in cuts:
        draws = jax.random.uniform(jax.random.fold_in(jax.random.fold_in(key, 6), position), (parts,), jnp.float32, least / len(cuts), top_value / len(cuts))
        level = level * jnp.repeat(jnp.exp(draws), extent[position] // parts).reshape((-1,) + (1,) * (len(extent) - 1 - position))
    return level


def gaussian(stream_key, extent, deviation, reach, cuts=(), kind=jnp.bfloat16):
    values = deviation * jax.random.normal(stream_key, extent, jnp.float32)
    if cuts:
        values = values * steps_of(stream_key, extent, cuts, -0.22, 0.18)
    return jnp.clip(values, -reach, reach).astype(kind)


def setup_inputs(seed: int = 0) -> dict:
    key_of = jax.random.split(jax.random.key(seed), 3)
    return {
        "train_grads": draw_train_grads(jax.random.fold_in(key_of[2], 71), 0),
        "targets": gaussian(key_of[1], (TARGETS, PROJ), 1.0, 6.0, ((0, 128),)),
    }


def solve_rows(factor, block):
    right = block.astype(jnp.float32)
    middle = lax.linalg.triangular_solve(factor, right, left_side=False, lower=True, transpose_a=True)
    result = lax.linalg.triangular_solve(factor, middle, left_side=False, lower=True, transpose_a=False)
    return result.astype(jnp.bfloat16)

def reference(train_grads, targets):
    gram = jnp.dot(train_grads.T.astype(jnp.float32), train_grads.astype(jnp.float32), preferred_element_type=jnp.float32)
    damping = 0.1 * jnp.trace(gram) / (TRAIN * PROJ)
    precond = gram / TRAIN + damping * jnp.eye(PROJ, dtype=jnp.float32)
    factor = jnp.linalg.cholesky(precond)
    solved = solve_rows(factor, targets)
    grads_blocks = train_grads.reshape(N_GRP, N_BLK, TR_DEV, PROJ).astype(jnp.float32)
    solved_blocks = solved.reshape(N_GRP, N_BLK, TGT_BLK, PROJ).astype(jnp.float32)
    pieces = []
    for step in range(VISITS):
        visiting = jnp.roll(solved_blocks, step, axis=1)
        pieces.append(jnp.einsum('gbrk,gbtk->gbrt', grads_blocks, visiting))
    joined = jnp.concatenate(pieces, axis=3) / jnp.sqrt(jnp.float32(PROJ))
    return joined.reshape(TRAIN, VISITS * TGT_BLK).astype(jnp.bfloat16)
```

```python
import functools

import jax
import jax.numpy as jnp
from jax import lax
from jax.experimental import pallas as pl
from jax.experimental.pallas import tpu as pltpu
from jax.sharding import PartitionSpec as P

VISITS = 3
NB = 128
TILE = 256
F32 = jnp.float32
BF16 = jnp.bfloat16


def wide(x):
    return jnp.broadcast_to(x, (8, NB))


def split2(x):
    hi = x.astype(BF16)
    return hi, (x - hi.astype(F32)).astype(BF16)


def split3(x):
    hi = x.astype(BF16)
    rest = x - hi.astype(F32)
    mid = rest.astype(BF16)
    return hi, mid, (rest - mid.astype(F32)).astype(BF16)


def dot(a, b):
    return jnp.dot(a, b, preferred_element_type=F32)


def dot3(a, b):
    ah, al = a
    bh, bl = b
    return dot(jnp.concatenate([ah, al], axis=1), jnp.concatenate([bh, bh], axis=0)) + dot(ah, bl)


PAIRS = ((0, 0), (0, 1), (1, 0), (1, 1), (0, 2), (2, 0))


def dot6(a, b):
    left = jnp.concatenate([a[p] for p, _ in PAIRS], axis=1)
    return dot(left, jnp.concatenate([b[q] for _, q in PAIRS], axis=0))


def outer6(a, b):
    a, b = split3(a), split3(b)
    left = jnp.concatenate([a[p] for p, _ in PAIRS], axis=0)
    right = jnp.concatenate([b[q] for _, q in PAIRS], axis=0)
    return lax.dot_general(left, right, (((0,), (0,)), ((), ())), preferred_element_type=F32)


def total(terms):
    while len(terms) > 1:
        terms = [terms[i] + terms[i + 1] for i in range(0, len(terms), 2)]
    return terms[0]


def pivot_rows(rows, k, buf):
    lane = lax.broadcasted_iota(jnp.int32, (8, NB), 1)
    sub = lax.broadcasted_iota(jnp.int32, (8, NB), 0)
    y = jnp.where((lane >= k) & (lane < k + 8), -(lane == sub + k).astype(F32), rows)
    for j in range(8):
        buf[j] = wide(rows[:, k + j : k + j + 1])
    m = [buf[j] for j in range(8)]
    for b in range(0, 8, 2):
        if b == 0:
            row = lambda i, j: wide(buf[j, i : i + 1, :])
        else:
            row = lambda i, j: wide(m[j][i : i + 1, :])
        e, f, g = row(b, b), row(b, b + 1), row(b + 1, b + 1)
        inv = 1.0 / (e * g - f * f)
        ie, jf, ig = g * inv, f * inv, e * inv
        left0 = jnp.where(sub == b, -1.0, jnp.where(sub == b + 1, 0.0, m[b]))
        left1 = jnp.where(sub == b + 1, -1.0, jnp.where(sub == b, 0.0, m[b + 1]))
        pair = (sub == b) | (sub == b + 1)

        def step(x, x0, x1):
            u0, u1 = ie * x0 - jf * x1, ig * x1 - jf * x0
            return jnp.where(pair, 0.0, x) - (left0 * u0 + left1 * u1)

        for j in range(b + 2, 8):
            m[j] = step(m[j], row(b, j), row(b + 1, j))
        y = step(y, wide(y[b : b + 1, :]), wide(y[b + 1 : b + 2, :]))
    return y


def neg_inverse(a, buf):
    lane = lax.broadcasted_iota(jnp.int32, (8, NB), 1)
    a = list(a)
    count = len(a)
    for g in range(count):
        k = 8 * g
        own = (lane >= k) & (lane < k + 8)
        rows = a[g]
        y = pivot_rows(rows, k, buf.at[g % 2])
        if g + 1 < count:
            t = a[g + 1]
            terms = [wide(t[:, k + j : k + j + 1]) * wide(y[j : j + 1, :]) for j in range(8)]
            a[g + 1] = jnp.where(own, 0.0, t) - total(terms)
        change = outer6(rows, y)
        for t in range(count):
            if t != g and t != g + 1:
                a[t] = jnp.where(own, 0.0, a[t]) - change[8 * t : 8 * t + 8, :]
        a[g] = y
    return a


def inverse(block, buf):
    block = 0.5 * (block + block.T)
    tiles = [block[8 * t : 8 * t + 8, :] for t in range(NB // 8)]
    return -jnp.concatenate(neg_inverse(tiles, buf), axis=0)


def solve_kernel(
    rows_total, gram_ref, right_ref, train_ref, out_ref, mat, left, buf, held, scored, x_ref, in_sem, out_sem
):
    width = gram_ref.shape[0]
    nblk = width // NB
    nrhs = right_ref.shape[0]
    rows = train_ref.shape[0]
    pieces = 8
    depth = rows // pieces
    load = pltpu.make_async_copy(train_ref, held, in_sem)
    load.start()

    eye = (lax.broadcasted_iota(jnp.int32, (NB, NB), 0) == lax.broadcasted_iota(jnp.int32, (NB, NB), 1)).astype(F32)
    diag = jnp.zeros((NB, NB), F32)
    for c in range(nblk):
        diag = diag + gram_ref[c * NB : (c + 1) * NB, c * NB : (c + 1) * NB] * eye
    trace = jnp.sum(jnp.sum(diag, axis=0, keepdims=True), axis=1, keepdims=True)
    damping = (0.1 * trace) / (rows_total * width)
    mat[:, :width] = gram_ref[...] * (1.0 / rows_total)
    for c in range(nblk):
        mat[c * NB : (c + 1) * NB, c * NB : (c + 1) * NB] += damping * eye
    for c in range(nrhs // NB):
        mat[:, width + c * NB : width + (c + 1) * NB] = right_ref[c * NB : (c + 1) * NB, :].astype(F32).T

    def step(j, _):
        here = pl.ds(pl.multiple_of(j * NB, NB), NB)
        inv = split3(inverse(mat[here, here], buf))
        inv = jnp.concatenate([inv[p] for p, _ in PAIRS], axis=1)
        hi, lo = split2(mat[:, here])
        left[:, :NB] = hi
        left[:, NB:] = lo

        def update(cols):
            row = split3(mat[here, cols])
            w = dot(inv, jnp.concatenate([row[q] for _, q in PAIRS], axis=0))
            wh, wl = split2(w)
            mat[:, cols] -= dot(left[...], jnp.concatenate([wh, wh], axis=0)) + dot(left[:, :NB], wl)
            mat[here, cols] = w

        lax.fori_loop((j + 1) // 2, width // TILE, lambda q, _: (update(pl.ds(pl.multiple_of(q * TILE, TILE), TILE)), 0)[1], 0)
        update(pl.ds(width, TILE))
        update(pl.ds(width + TILE, nrhs - TILE))
        return 0

    lax.fori_loop(0, nblk, step, 0)
    x_ref[...] = mat[:, width:].astype(BF16)
    load.wait()
    scale = 1.0 / (width ** 0.5)

    def score(p, _):
        part = pl.ds(pl.multiple_of(p * depth, depth), depth)
        scored[part, :] = (dot(held[part, :], x_ref[...]) * scale).astype(BF16)
        pltpu.make_async_copy(scored.at[part], out_ref.at[part], out_sem).start()
        return 0

    lax.fori_loop(0, pieces, score, 0)
    pltpu.make_async_copy(scored, out_ref, out_sem).wait()


def solve_and_score(gram, right, train, rows_total):
    width = gram.shape[0]
    rows = train.shape[0]
    nrhs = right.shape[0]
    return pl.pallas_call(
        functools.partial(solve_kernel, rows_total),
        out_shape=jax.ShapeDtypeStruct((rows, nrhs), BF16),
        in_specs=[
            pl.BlockSpec(memory_space=pltpu.VMEM),
            pl.BlockSpec(memory_space=pltpu.VMEM),
            pl.BlockSpec(memory_space=pl.ANY),
        ],
        out_specs=pl.BlockSpec(memory_space=pl.ANY),
        scratch_shapes=[
            pltpu.VMEM((width, width + nrhs), F32),
            pltpu.VMEM((width, 2 * NB), BF16),
            pltpu.VMEM((2, 8, 8, NB), F32),
            pltpu.VMEM((rows, width), BF16),
            pltpu.VMEM((rows, nrhs), BF16),
            pltpu.VMEM((width, nrhs), BF16),
            pltpu.SemaphoreType.DMA,
            pltpu.SemaphoreType.DMA,
        ],
        compiler_params=pltpu.CompilerParams(vmem_limit_bytes=56 << 20),
        name="solve_and_score",
    )(gram, right, train)


def passed_along(value, axis, steps):
    count = lax.axis_size(axis)
    pairs = [(source, (source + steps) % count) for source in range(count)]
    return lax.ppermute(value, axis, pairs)


def per_device(train_grads, targets):
    rows_total = train_grads.shape[0] * lax.axis_size("grp") * lax.axis_size("blk")
    visiting = [targets]
    for step in range(1, VISITS):
        visiting.append(passed_along(targets, "blk", step))
    right = jnp.concatenate(visiting, axis=0)
    local_gram = lax.dot_general(train_grads, train_grads, (((0,), (0,)), ((), ())), preferred_element_type=F32)
    gram = lax.psum(local_gram, ("grp", "blk"))
    return solve_and_score(gram, right, train_grads, rows_total)


def solution(mesh):
    spec = P(("grp", "blk"), None)
    return jax.shard_map(per_device, mesh=mesh, in_specs=(spec, spec), out_specs=spec, check_vma=False)
```

```python
import functools

import jax
import jax.numpy as jnp
from jax import lax
from jax.experimental import pallas as pl
from jax.experimental.pallas import tpu as pltpu
from jax.sharding import PartitionSpec as P

VISITS = 3
NB = 128
TILE = 256
F32 = jnp.float32
BF16 = jnp.bfloat16
MESH = pl.DeviceIdType.MESH


def upper_blocks(count):
    first = [i for i in range(count) if i < 2 or i >= count - 2]
    rest = [i for i in range(count) if 2 <= i < count - 2]
    return [(i, c) for i in first + rest for c in range(i, count)]


def wide(x):
    return jnp.broadcast_to(x, (8, NB))


def split2(x):
    hi = x.astype(BF16)
    return hi, (x - hi.astype(F32)).astype(BF16)


def split3(x):
    hi = x.astype(BF16)
    rest = x - hi.astype(F32)
    mid = rest.astype(BF16)
    return hi, mid, (rest - mid.astype(F32)).astype(BF16)


def dot(a, b):
    return jnp.dot(a, b, preferred_element_type=F32)


def dot3(a, b):
    ah, al = a
    bh, bl = b
    return dot(jnp.concatenate([ah, al], axis=1), jnp.concatenate([bh, bh], axis=0)) + dot(ah, bl)


PAIRS = ((0, 0), (0, 1), (1, 0), (1, 1), (0, 2), (2, 0))


def dot6(a, b):
    left = jnp.concatenate([a[p] for p, _ in PAIRS], axis=1)
    return dot(left, jnp.concatenate([b[q] for _, q in PAIRS], axis=0))


def outer6(a, b):
    a, b = split3(a), split3(b)
    left = jnp.concatenate([a[p] for p, _ in PAIRS], axis=0)
    right = jnp.concatenate([b[q] for _, q in PAIRS], axis=0)
    return lax.dot_general(left, right, (((0,), (0,)), ((), ())), preferred_element_type=F32)


def total(terms):
    while len(terms) > 1:
        terms = [terms[i] + terms[i + 1] for i in range(0, len(terms), 2)]
    return terms[0]


def pivot_rows(rows, k, buf):
    lane = lax.broadcasted_iota(jnp.int32, (8, NB), 1)
    sub = lax.broadcasted_iota(jnp.int32, (8, NB), 0)
    y = jnp.where((lane >= k) & (lane < k + 8), -(lane == sub + k).astype(F32), rows)
    for j in range(8):
        buf[j] = wide(rows[:, k + j : k + j + 1])
    m = [buf[j] for j in range(8)]
    for b in range(0, 8, 2):
        if b == 0:
            row = lambda i, j: wide(buf[j, i : i + 1, :])
        else:
            row = lambda i, j: wide(m[j][i : i + 1, :])
        e, f, g = row(b, b), row(b, b + 1), row(b + 1, b + 1)
        inv = 1.0 / (e * g - f * f)
        ie, jf, ig = g * inv, f * inv, e * inv
        left0 = jnp.where(sub == b, -1.0, jnp.where(sub == b + 1, 0.0, m[b]))
        left1 = jnp.where(sub == b + 1, -1.0, jnp.where(sub == b, 0.0, m[b + 1]))
        pair = (sub == b) | (sub == b + 1)

        def step(x, x0, x1):
            u0, u1 = ie * x0 - jf * x1, ig * x1 - jf * x0
            return jnp.where(pair, 0.0, x) - (left0 * u0 + left1 * u1)

        for j in range(b + 2, 8):
            m[j] = step(m[j], row(b, j), row(b + 1, j))
        y = step(y, wide(y[b : b + 1, :]), wide(y[b + 1 : b + 2, :]))
    return y


def neg_inverse(a, buf):
    lane = lax.broadcasted_iota(jnp.int32, (8, NB), 1)
    a = list(a)
    count = len(a)
    for g in range(count):
        k = 8 * g
        own = (lane >= k) & (lane < k + 8)
        rows = a[g]
        y = pivot_rows(rows, k, buf.at[g % 2])
        if g + 1 < count:
            t = a[g + 1]
            terms = [wide(t[:, k + j : k + j + 1]) * wide(y[j : j + 1, :]) for j in range(8)]
            a[g + 1] = jnp.where(own, 0.0, t) - total(terms)
        change = outer6(rows, y)
        for t in range(count):
            if t != g and t != g + 1:
                a[t] = jnp.where(own, 0.0, a[t]) - change[8 * t : 8 * t + 8, :]
        a[g] = y
    return a


def inverse(block, buf):
    block = 0.5 * (block + block.T)
    tiles = [block[8 * t : 8 * t + 8, :] for t in range(NB // 8)]
    return -jnp.concatenate(neg_inverse(tiles, buf), axis=0)


def solve_kernel(
    rows_total, gram_ref, right_ref, train_ref, out_ref, mat, left, buf, held, scored, x_ref, in_sem, out_sem
):
    width = right_ref.shape[1]
    nblk = width // NB
    nrhs = right_ref.shape[0]
    rows = train_ref.shape[0]
    pieces = 8
    depth = rows // pieces
    load = pltpu.make_async_copy(train_ref, held, in_sem)
    load.start()

    eye = (lax.broadcasted_iota(jnp.int32, (NB, NB), 0) == lax.broadcasted_iota(jnp.int32, (NB, NB), 1)).astype(F32)
    blocks = upper_blocks(nblk)
    diag = jnp.zeros((NB, NB), F32)
    for n, (i, c) in enumerate(blocks):
        if i == c:
            diag = diag + gram_ref[n * NB : (n + 1) * NB, :] * eye
    trace = jnp.sum(jnp.sum(diag, axis=0, keepdims=True), axis=1, keepdims=True)
    damping = (0.1 * trace) / (rows_total * width)
    for n, (i, c) in enumerate(blocks):
        block = gram_ref[n * NB : (n + 1) * NB, :] * (1.0 / rows_total)
        if i == c:
            mat[i * NB : (i + 1) * NB, i * NB : (i + 1) * NB] = block + damping * eye
        else:
            mat[i * NB : (i + 1) * NB, c * NB : (c + 1) * NB] = block
            mat[c * NB : (c + 1) * NB, i * NB : (i + 1) * NB] = block.T
    for c in range(nrhs // NB):
        mat[:, width + c * NB : width + (c + 1) * NB] = right_ref[c * NB : (c + 1) * NB, :].astype(F32).T

    def step(j, _):
        here = pl.ds(pl.multiple_of(j * NB, NB), NB)
        inv = split3(inverse(mat[here, here], buf))
        inv = jnp.concatenate([inv[p] for p, _ in PAIRS], axis=1)
        hi, lo = split2(mat[:, here])
        left[:, :NB] = hi
        left[:, NB:] = lo

        def update(cols):
            row = split3(mat[here, cols])
            w = dot(inv, jnp.concatenate([row[q] for _, q in PAIRS], axis=0))
            wh, wl = split2(w)
            mat[:, cols] -= dot(left[...], jnp.concatenate([wh, wh], axis=0)) + dot(left[:, :NB], wl)
            mat[here, cols] = w

        lax.fori_loop((j + 1) // 2, width // TILE, lambda q, _: (update(pl.ds(pl.multiple_of(q * TILE, TILE), TILE)), 0)[1], 0)
        update(pl.ds(width, TILE))
        update(pl.ds(width + TILE, nrhs - TILE))
        return 0

    lax.fori_loop(0, nblk, step, 0)
    x_ref[...] = mat[:, width:].astype(BF16)
    load.wait()
    scale = 1.0 / (width ** 0.5)

    def score(p, _):
        part = pl.ds(pl.multiple_of(p * depth, depth), depth)
        scored[part, :] = (dot(held[part, :], x_ref[...]) * scale).astype(BF16)
        pltpu.make_async_copy(scored.at[part], out_ref.at[part], out_sem).start()
        return 0

    lax.fori_loop(0, pieces, score, 0)
    pltpu.make_async_copy(scored, out_ref, out_sem).wait()


def solve_and_score(gram, right, train, rows_total):
    rows, width = train.shape
    nrhs = right.shape[0]
    return pl.pallas_call(
        functools.partial(solve_kernel, rows_total),
        out_shape=jax.ShapeDtypeStruct((rows, nrhs), BF16),
        in_specs=[
            pl.BlockSpec(memory_space=pltpu.VMEM),
            pl.BlockSpec(memory_space=pltpu.VMEM),
            pl.BlockSpec(memory_space=pl.ANY),
        ],
        out_specs=pl.BlockSpec(memory_space=pl.ANY),
        scratch_shapes=[
            pltpu.VMEM((width, width + nrhs), F32),
            pltpu.VMEM((width, 2 * NB), BF16),
            pltpu.VMEM((2, 8, 8, NB), F32),
            pltpu.VMEM((rows, width), BF16),
            pltpu.VMEM((rows, nrhs), BF16),
            pltpu.VMEM((width, nrhs), BF16),
            pltpu.SemaphoreType.DMA,
            pltpu.SemaphoreType.DMA,
        ],
        compiler_params=pltpu.CompilerParams(vmem_limit_bytes=56 << 20),
        name="solve_and_score",
    )(gram, right, train)


def gram_kernel(train_ref, out_ref, held, sems):
    width = held.shape[1]
    chunks = sems.shape[0]
    depth = held.shape[0] // chunks
    loads = [
        pltpu.make_async_copy(train_ref.at[pl.ds(k * depth, depth)], held.at[pl.ds(k * depth, depth)], sems.at[k])
        for k in range(chunks)
    ]
    for load in loads:
        load.start()
    place = {key: n for n, key in enumerate(upper_blocks(width // NB))}
    for k in range(chunks):
        loads[k].wait()
        for first in range(0, width // NB, 2):
            part = held[k * depth : (k + 1) * depth, first * NB :]
            res = lax.dot_general(part[:, : 2 * NB], part, (((0,), (0,)), ((), ())), preferred_element_type=F32)
            for i in (first, first + 1):
                for c in range(i, width // NB):
                    n = place[i, c]
                    block = res[(i - first) * NB : (i - first + 1) * NB, (c - first) * NB : (c - first + 1) * NB]
                    if k == 0:
                        out_ref[n * NB : (n + 1) * NB, :] = block
                    else:
                        out_ref[n * NB : (n + 1) * NB, :] += block


def packed_gram(train):
    rows, width = train.shape
    count = len(upper_blocks(width // NB))
    return pl.pallas_call(
        gram_kernel,
        out_shape=jax.ShapeDtypeStruct((count * NB, NB), F32),
        in_specs=[pl.BlockSpec(memory_space=pl.ANY)],
        out_specs=pl.BlockSpec(memory_space=pltpu.VMEM),
        scratch_shapes=[pltpu.VMEM((rows, width), BF16), pltpu.SemaphoreType.DMA((4,))],
        compiler_params=pltpu.CompilerParams(vmem_limit_bytes=56 << 20),
        name="packed_gram",
    )(train)


RING = 4
PARTS = 3


def sum_kernel(
    gram_ref, target_ref, out_ref, right_ref, pair, work, got1, sum1, got2, sum2, got3, full2,
    send0, recv0, send1, recv1, send2, recv2, send3, recv3, send4, recv4, send5, recv5, send6, recv6, send7, recv7, own_sem,
):
    grp, blk = lax.axis_index("grp"), lax.axis_index("blk")
    core = lax.rem(grp, 2)
    pos = (lax.rem(blk, 2) * 2 + grp // 2, blk // 8, lax.rem(blk // 2, RING))

    def device(where, which):
        x, y, z = where
        return (lax.rem(x, 2) * 2 + which, (y * RING + z) * 2 + x // 2)

    def along(axis, d):
        where = list(pos)
        where[axis] = lax.rem(where[axis] + d, RING)
        return device(where, core)

    mate = device(pos, 1 - core)
    blks = lax.axis_size("blk")
    ahead = [(grp, lax.rem(blk + s, blks)) for s in range(1, VISITS)]
    behind = [(grp, lax.rem(blk + blks - s, blks)) for s in range(1, VISITS)]
    mates = [mate] + [along(axis, d) for axis in range(3) for d in range(1, RING)]

    barrier = pltpu.get_barrier_semaphore()
    for other in mates + behind:
        pl.semaphore_signal(barrier, inc=1, device_id=other, device_id_type=MESH)
    pl.semaphore_wait(barrier, len(mates) + len(ahead))

    def remote(src, dst, send, recv, who):
        return pltpu.make_async_remote_copy(
            src_ref=src, dst_ref=dst, send_sem=send, recv_sem=recv, device_id=who, device_id_type=MESH
        )

    half = gram_ref.shape[0] // 2
    third = half // PARTS
    q1 = third // RING
    q2 = q1 // RING

    def rows(start, size):
        return pl.ds(pl.multiple_of(start, 8), size)

    c0, c1, c2, c3, c4, c5, c6, c7 = {}, {}, {}, {}, {}, {}, {}, {}
    for p in range(PARTS):
        c0[p] = remote(
            gram_ref.at[rows((1 - core) * half + p * third, third)], pair.at[p], send0.at[p], recv0.at[p], mate
        )
        c0[p].start()
    nt = target_ref.shape[0]
    for s in range(1, VISITS):
        c7[s] = remote(target_ref, right_ref.at[pl.ds(s * nt, nt)], send7.at[s - 1], recv7.at[s - 1], ahead[s - 1])
        c7[s].start()
    right_ref[0:nt, :] = target_ref[...]

    steps = range(1, RING)
    for p in range(PARTS):
        axis = p
        c0[p].wait_recv()
        work[p] = gram_ref[rows(core * half + p * third, third), :] + pair[p]
        for d in steps:
            c1[p, d] = remote(
                work.at[p, rows(lax.rem(pos[axis] + d, RING) * q1, q1)],
                got1.at[p, d - 1], send1.at[p, d - 1], recv1.at[p, d - 1], along(axis, d),
            )
            c1[p, d].start()
    for p in range(PARTS):
        axis = (p + 1) % 3
        for d in steps:
            c1[p, d].wait_recv()
        mine = work[p, rows(pos[p] * q1, q1), :]
        sum1[p] = (mine + got1[p, 0]) + (got1[p, 1] + got1[p, 2])
        for d in steps:
            c2[p, d] = remote(
                sum1.at[p, rows(lax.rem(pos[axis] + d, RING) * q2, q2)],
                got2.at[p, d - 1], send2.at[p, d - 1], recv2.at[p, d - 1], along(axis, d),
            )
            c2[p, d].start()
    for p in range(PARTS):
        axis = (p + 2) % 3
        for d in steps:
            c2[p, d].wait_recv()
        mine = sum1[p, rows(pos[(p + 1) % 3] * q2, q2), :]
        sum2[p] = (mine + got2[p, 0]) + (got2[p, 1] + got2[p, 2])
        for d in steps:
            c3[p, d] = remote(sum2.at[p], got3.at[p, d - 1], send3.at[p, d - 1], recv3.at[p, d - 1], along(axis, d))
            c3[p, d].start()
    for p in range(PARTS):
        axis = (p + 1) % 3
        for d in steps:
            c3[p, d].wait_recv()
        spot = rows(pos[axis] * q2, q2)
        full2[p, spot, :] = (sum2[p] + got3[p, 0]) + (got3[p, 1] + got3[p, 2])
        for d in steps:
            c4[p, d] = remote(
                full2.at[p, spot], full2.at[p, spot], send4.at[p, d - 1], recv4.at[p, d - 1], along(axis, d)
            )
            c4[p, d].start()
    own = []
    for p in range(PARTS):
        for d in steps:
            c4[p, d].wait_recv()
        spot = rows(core * half + p * third + pos[p] * q1, q1)
        for d in steps:
            c5[p, d] = remote(full2.at[p], out_ref.at[spot], send5.at[p, d - 1], recv5.at[p, d - 1], along(p, d))
            c5[p, d].start()
        c6[p, 0] = remote(full2.at[p], out_ref.at[spot], send6.at[p, 0], recv6.at[p, 0], mate)
        c6[p, 0].start()
        own.append(pltpu.make_async_copy(full2.at[p], out_ref.at[spot], own_sem.at[p]))
        own[-1].start()
    for d in (1, 3, 2):
        for p in range(PARTS):
            c5[p, d].wait_recv()
            spot = rows(core * half + p * third + lax.rem(pos[p] + RING - d, RING) * q1, q1)
            c6[p, d] = remote(out_ref.at[spot], out_ref.at[spot], send6.at[p, d], recv6.at[p, d], mate)
            c6[p, d].start()
    for copies in (c0, c1, c2, c3, c4, c5, c6, c7):
        for copy in copies.values():
            copy.wait_send()
    for copy in own:
        copy.wait()
    for copies in (c6, c7):
        for copy in copies.values():
            copy.wait_recv()


def summed_over_devices(gram, targets):
    total_rows = gram.shape[0]
    third = total_rows // (2 * PARTS)
    q1, q2 = third // RING, third // (RING * RING)
    sem = pltpu.SemaphoreType.DMA
    fan = RING - 1
    pairs = [(PARTS,)] + [(PARTS, fan)] * 5 + [(PARTS, RING), (VISITS - 1,)]
    return pl.pallas_call(
        sum_kernel,
        out_shape=(
            jax.ShapeDtypeStruct(gram.shape, F32),
            jax.ShapeDtypeStruct((VISITS * targets.shape[0], targets.shape[1]), BF16),
        ),
        in_specs=[pl.BlockSpec(memory_space=pltpu.VMEM)] * 2,
        out_specs=[pl.BlockSpec(memory_space=pltpu.VMEM)] * 2,
        scratch_shapes=[
            pltpu.VMEM((PARTS, third, NB), F32),
            pltpu.VMEM((PARTS, third, NB), F32),
            pltpu.VMEM((PARTS, fan, q1, NB), F32),
            pltpu.VMEM((PARTS, q1, NB), F32),
            pltpu.VMEM((PARTS, fan, q2, NB), F32),
            pltpu.VMEM((PARTS, q2, NB), F32),
            pltpu.VMEM((PARTS, fan, q2, NB), F32),
            pltpu.VMEM((PARTS, q1, NB), F32),
        ]
        + [sem(shape) for shape in pairs for _ in range(2)]
        + [sem((PARTS,))],
        compiler_params=pltpu.CompilerParams(
            collective_id=0, has_side_effects=True, vmem_limit_bytes=56 << 20
        ),
        name="summed_over_devices",
    )(gram, targets)


def per_device(train_grads, targets):
    rows_total = train_grads.shape[0] * lax.axis_size("grp") * lax.axis_size("blk")
    gram, right = summed_over_devices(packed_gram(train_grads), targets)
    return solve_and_score(gram, right, train_grads, rows_total)


def solution(mesh):
    spec = P(("grp", "blk"), None)
    return jax.shard_map(per_device, mesh=mesh, in_specs=(spec, spec), out_specs=spec, check_vma=False)
```

```python
import functools

import jax
import jax.numpy as jnp
from jax import lax
from jax.experimental import pallas as pl
from jax.experimental.pallas import tpu as pltpu
from jax.sharding import PartitionSpec as P

VISITS = 3
NB = 128
TILE = 256
UNROLLED = True
F32 = jnp.float32
BF16 = jnp.bfloat16
MESH = pl.DeviceIdType.MESH


def panels(count):
    wide_count = count // 2
    order = [n for n in range(wide_count)]
    return [[order[-1], order[0]], order[1:-1][::-1]]


def upper_blocks(count):
    return [
        (i, c) for half in panels(count) for panel in half for c in (2 * panel, 2 * panel + 1) for i in range(c + 1)
    ]


def wide(x):
    return jnp.broadcast_to(x, (8, NB))


def split2(x):
    hi = x.astype(BF16)
    return hi, (x - hi.astype(F32)).astype(BF16)


def split3(x):
    hi = x.astype(BF16)
    rest = x - hi.astype(F32)
    mid = rest.astype(BF16)
    return hi, mid, (rest - mid.astype(F32)).astype(BF16)


def dot(a, b):
    return jnp.dot(a, b, preferred_element_type=F32)


def dot3(a, b):
    ah, al = a
    bh, bl = b
    return dot(jnp.concatenate([ah, al], axis=1), jnp.concatenate([bh, bh], axis=0)) + dot(ah, bl)


PAIRS = ((0, 0), (0, 1), (1, 0), (1, 1), (0, 2), (2, 0))


def dot6(a, b):
    left = jnp.concatenate([a[p] for p, _ in PAIRS], axis=1)
    return dot(left, jnp.concatenate([b[q] for _, q in PAIRS], axis=0))


def outer6(a, b):
    a, b = split3(a), split3(b)
    left = jnp.concatenate([a[p] for p, _ in PAIRS], axis=0)
    right = jnp.concatenate([b[q] for _, q in PAIRS], axis=0)
    return lax.dot_general(left, right, (((0,), (0,)), ((), ())), preferred_element_type=F32)


def total(terms):
    while len(terms) > 1:
        terms = [terms[i] + terms[i + 1] for i in range(0, len(terms), 2)]
    return terms[0]


def pivot_rows(rows, k, buf):
    lane = lax.broadcasted_iota(jnp.int32, (8, NB), 1)
    sub = lax.broadcasted_iota(jnp.int32, (8, NB), 0)
    y = jnp.where((lane >= k) & (lane < k + 8), -(lane == sub + k).astype(F32), rows)
    for j in range(8):
        buf[j] = wide(rows[:, k + j : k + j + 1])
    m = [buf[j] for j in range(8)]
    for b in range(0, 8, 2):
        if b == 0:
            row = lambda i, j: wide(buf[j, i : i + 1, :])
        else:
            row = lambda i, j: wide(m[j][i : i + 1, :])
        e, f, g = row(b, b), row(b, b + 1), row(b + 1, b + 1)
        inv = 1.0 / (e * g - f * f)
        ie, jf, ig = g * inv, f * inv, e * inv
        left0 = jnp.where(sub == b, -1.0, jnp.where(sub == b + 1, 0.0, m[b]))
        left1 = jnp.where(sub == b + 1, -1.0, jnp.where(sub == b, 0.0, m[b + 1]))
        pair = (sub == b) | (sub == b + 1)

        def step(x, x0, x1):
            u0, u1 = ie * x0 - jf * x1, ig * x1 - jf * x0
            return jnp.where(pair, 0.0, x) - (left0 * u0 + left1 * u1)

        for j in range(b + 2, 8):
            m[j] = step(m[j], row(b, j), row(b + 1, j))
        y = step(y, wide(y[b : b + 1, :]), wide(y[b + 1 : b + 2, :]))
    return y


def neg_inverse(a, buf):
    lane = lax.broadcasted_iota(jnp.int32, (8, NB), 1)
    a = list(a)
    count = len(a)
    for g in range(count):
        k = 8 * g
        own = (lane >= k) & (lane < k + 8)
        rows = a[g]
        y = pivot_rows(rows, k, buf.at[g % 2])
        if g + 1 < count:
            t = a[g + 1]
            terms = [wide(t[:, k + j : k + j + 1]) * wide(y[j : j + 1, :]) for j in range(8)]
            a[g + 1] = jnp.where(own, 0.0, t) - total(terms)
        change = outer6(rows, y)
        for t in range(count):
            if t != g and t != g + 1:
                a[t] = jnp.where(own, 0.0, a[t]) - change[8 * t : 8 * t + 8, :]
        a[g] = y
    return a


def inverse(block, buf):
    block = 0.5 * (block + block.T)
    tiles = [block[8 * t : 8 * t + 8, :] for t in range(NB // 8)]
    return -jnp.concatenate(neg_inverse(tiles, buf), axis=0)


def solve_kernel(
    rows_total, gram_ref, right_ref, train_ref, out_ref, mat, left, right, panel, buf, held, scored, x_ref, in_sem, out_sem
):
    width = right_ref.shape[1]
    nblk = width // NB
    nrhs = right_ref.shape[0]
    rows = train_ref.shape[0]
    pieces = 8
    depth = rows // pieces
    load = pltpu.make_async_copy(train_ref, held, in_sem)
    load.start()

    eye = (lax.broadcasted_iota(jnp.int32, (NB, NB), 0) == lax.broadcasted_iota(jnp.int32, (NB, NB), 1)).astype(F32)
    blocks = upper_blocks(nblk)
    diag = jnp.zeros((NB, NB), F32)
    for n, (i, c) in enumerate(blocks):
        if i == c:
            diag = diag + gram_ref[n * NB : (n + 1) * NB, :] * eye
    trace = jnp.sum(jnp.sum(diag, axis=0, keepdims=True), axis=1, keepdims=True)
    damping = (0.1 * trace) / (rows_total * width)
    for n, (i, c) in enumerate(blocks):
        block = gram_ref[n * NB : (n + 1) * NB, :] * (1.0 / rows_total)
        if i == c:
            mat[i * NB : (i + 1) * NB, i * NB : (i + 1) * NB] = block + damping * eye
        else:
            mat[i * NB : (i + 1) * NB, c * NB : (c + 1) * NB] = block
            mat[c * NB : (c + 1) * NB, i * NB : (i + 1) * NB] = block.T
    for c in range(nrhs // NB):
        mat[:, width + c * NB : width + (c + 1) * NB] = right_ref[c * NB : (c + 1) * NB, :].astype(F32).T

    def step(j, start):
        here = pl.ds(j * NB if isinstance(j, int) else pl.multiple_of(j * NB, NB), NB)
        tiles = [(c, min(c + TILE, width + nrhs)) for c in range(start, width + nrhs, TILE)]
        inv = split3(inverse(mat[here, here], buf))
        inv = jnp.concatenate([inv[p] for p, _ in PAIRS], axis=1)
        hi, lo = split2(mat[:, here])
        left[:, :NB] = hi
        left[:, NB : 2 * NB] = lo
        left[:, 2 * NB :] = hi
        for lo_col, hi_col in tiles:
            row = split3(mat[here, lo_col:hi_col])
            w = dot(inv, jnp.concatenate([row[q] for _, q in PAIRS], axis=0))
            wh, wl = split2(w)
            for n, part in enumerate((wh, wh, wl)):
                right[n * NB : (n + 1) * NB, lo_col:hi_col] = part
            panel[:, lo_col:hi_col] = w
        for lo_col, hi_col in tiles:
            mat[:, lo_col:hi_col] -= dot(left[...], right[:, lo_col:hi_col])
        for lo_col, hi_col in tiles:
            mat[here, lo_col:hi_col] = panel[:, lo_col:hi_col]

    if UNROLLED:
        for j in range(nblk):
            step(j, (j + 1) * NB)
    else:
        for s in range(0, nblk, 2):
            lax.fori_loop(s, s + 2, lambda j, _, s=s: (step(j, s * NB), 0)[1], 0)
    x_ref[...] = mat[:, width:].astype(BF16)
    load.wait()
    scale = 1.0 / (width ** 0.5)

    def score(p, _):
        part = pl.ds(pl.multiple_of(p * depth, depth), depth)
        scored[part, :] = (dot(held[part, :], x_ref[...]) * scale).astype(BF16)
        pltpu.make_async_copy(scored.at[part], out_ref.at[part], out_sem).start()
        return 0

    lax.fori_loop(0, pieces, score, 0)
    pltpu.make_async_copy(scored, out_ref, out_sem).wait()


def solve_and_score(gram, right, train, rows_total):
    rows, width = train.shape
    nrhs = right.shape[0]
    return pl.pallas_call(
        functools.partial(solve_kernel, rows_total),
        out_shape=jax.ShapeDtypeStruct((rows, nrhs), BF16),
        in_specs=[
            pl.BlockSpec(memory_space=pltpu.VMEM),
            pl.BlockSpec(memory_space=pltpu.VMEM),
            pl.BlockSpec(memory_space=pl.ANY),
        ],
        out_specs=pl.BlockSpec(memory_space=pl.ANY),
        scratch_shapes=[
            pltpu.VMEM((width, width + nrhs), F32),
            pltpu.VMEM((width, 3 * NB), BF16),
            pltpu.VMEM((3 * NB, width + nrhs), BF16),
            pltpu.VMEM((NB, width + nrhs), F32),
            pltpu.VMEM((2, 8, 8, NB), F32),
            pltpu.VMEM((rows, width), BF16),
            pltpu.VMEM((rows, nrhs), BF16),
            pltpu.VMEM((width, nrhs), BF16),
            pltpu.SemaphoreType.DMA,
            pltpu.SemaphoreType.DMA,
        ],
        compiler_params=pltpu.CompilerParams(vmem_limit_bytes=56 << 20),
        name="solve_and_score",
    )(gram, right, train)


RING = 4
PARTS = 3


def gram_panel(panel, held, gram, loads, place):
    rows = held.shape[0]
    depth = rows // len(loads)
    for k, load in enumerate(loads):
        if load is not None:
            load.wait()
        part = held[k * depth : (k + 1) * depth, : (panel + 1) * 2 * NB]
        res = lax.dot_general(part, part[:, panel * 2 * NB :], (((0,), (0,)), ((), ())), preferred_element_type=F32)
        for n in range(2):
            c = 2 * panel + n
            for i in range(c + 1):
                spot = slice(place[i, c] * NB, place[i, c] * NB + NB)
                block = res[i * NB : (i + 1) * NB, n * NB : (n + 1) * NB]
                if k == 0:
                    gram[spot, :] = block
                else:
                    gram[spot, :] += block


def sum_kernel(
    train_ref, target_ref, out_ref, right_ref, held, gram_ref, pair, work, got1, sum1, got2, sum2, got3, full2,
    send0, recv0, send1, recv1, send2, recv2, send3, recv3, send4, recv4, send5, recv5, send6, recv6, send7, recv7,
    own_sem, load_sem,
):
    chunks = load_sem.shape[0]
    depth = held.shape[0] // chunks
    loads = [
        pltpu.make_async_copy(train_ref.at[pl.ds(k * depth, depth)], held.at[pl.ds(k * depth, depth)], load_sem.at[k])
        for k in range(chunks)
    ]
    for load in loads:
        load.start()
    nblk = held.shape[1] // NB
    halves = panels(nblk)
    place = {key: n for n, key in enumerate(upper_blocks(nblk))}
    grp, blk = lax.axis_index("grp"), lax.axis_index("blk")
    core = lax.rem(grp, 2)
    pos = (lax.rem(blk, 2) * 2 + grp // 2, blk // 8, lax.rem(blk // 2, RING))

    def device(where, which):
        x, y, z = where
        return (lax.rem(x, 2) * 2 + which, (y * RING + z) * 2 + x // 2)

    def along(axis, d):
        where = list(pos)
        where[axis] = lax.rem(where[axis] + d, RING)
        return device(where, core)

    mate = device(pos, 1 - core)
    blks = lax.axis_size("blk")
    ahead = [(grp, lax.rem(blk + s, blks)) for s in range(1, VISITS)]
    behind = [(grp, lax.rem(blk + blks - s, blks)) for s in range(1, VISITS)]
    mates = [mate] + [along(axis, d) for axis in range(3) for d in range(1, RING)]

    barrier = pltpu.get_barrier_semaphore()
    for other in mates + behind:
        pl.semaphore_signal(barrier, inc=1, device_id=other, device_id_type=MESH)

    done = [None] * chunks
    for c in range(2):

        @pl.when(core == c)
        def _():
            for n, panel in enumerate(halves[1 - c]):
                gram_panel(panel, held, gram_ref, done if n else loads, place)

    pl.semaphore_wait(barrier, len(mates) + len(ahead))

    def remote(src, dst, send, recv, who):
        return pltpu.make_async_remote_copy(
            src_ref=src, dst_ref=dst, send_sem=send, recv_sem=recv, device_id=who, device_id_type=MESH
        )

    half = gram_ref.shape[0] // 2
    third = half // PARTS
    q1 = third // RING
    q2 = q1 // RING

    def rows(start, size):
        return pl.ds(pl.multiple_of(start, 8), size)

    c0, c1, c2, c3, c4, c5, c6, c7 = {}, {}, {}, {}, {}, {}, {}, {}
    for p in range(PARTS):
        c0[p] = remote(
            gram_ref.at[rows((1 - core) * half + p * third, third)], pair.at[p], send0.at[p], recv0.at[p], mate
        )
        c0[p].start()
    nt = target_ref.shape[0]
    for s in range(1, VISITS):
        c7[s] = remote(target_ref, right_ref.at[pl.ds(s * nt, nt)], send7.at[s - 1], recv7.at[s - 1], ahead[s - 1])
        c7[s].start()
    own = [pltpu.make_async_copy(target_ref, right_ref.at[pl.ds(0, nt)], own_sem.at[PARTS])]
    own[0].start()
    for c in range(2):

        @pl.when(core == c)
        def _():
            for panel in halves[c]:
                gram_panel(panel, held, gram_ref, done, place)

    steps = range(1, RING)
    for p in range(PARTS):
        axis = p
        c0[p].wait_recv()
        work[p] = gram_ref[rows(core * half + p * third, third), :] + pair[p]
        for d in steps:
            c1[p, d] = remote(
                work.at[p, rows(lax.rem(pos[axis] + d, RING) * q1, q1)],
                got1.at[p, d - 1], send1.at[p, d - 1], recv1.at[p, d - 1], along(axis, d),
            )
            c1[p, d].start()
    for p in range(PARTS):
        axis = (p + 1) % 3
        for d in steps:
            c1[p, d].wait_recv()
        mine = work[p, rows(pos[p] * q1, q1), :]
        sum1[p] = (mine + got1[p, 0]) + (got1[p, 1] + got1[p, 2])
        for d in steps:
            c2[p, d] = remote(
                sum1.at[p, rows(lax.rem(pos[axis] + d, RING) * q2, q2)],
                got2.at[p, d - 1], send2.at[p, d - 1], recv2.at[p, d - 1], along(axis, d),
            )
            c2[p, d].start()
    for p in range(PARTS):
        axis = (p + 2) % 3
        for d in steps:
            c2[p, d].wait_recv()
        mine = sum1[p, rows(pos[(p + 1) % 3] * q2, q2), :]
        sum2[p] = (mine + got2[p, 0]) + (got2[p, 1] + got2[p, 2])
        for d in steps:
            c3[p, d] = remote(sum2.at[p], got3.at[p, d - 1], send3.at[p, d - 1], recv3.at[p, d - 1], along(axis, d))
            c3[p, d].start()
    for p in range(PARTS):
        axis = (p + 1) % 3
        for d in steps:
            c3[p, d].wait_recv()
        spot = rows(pos[axis] * q2, q2)
        full2[p, spot, :] = (sum2[p] + got3[p, 0]) + (got3[p, 1] + got3[p, 2])
        for d in steps:
            c4[p, d] = remote(
                full2.at[p, spot], full2.at[p, spot], send4.at[p, d - 1], recv4.at[p, d - 1], along(axis, d)
            )
            c4[p, d].start()
    for p in range(PARTS):
        for d in steps:
            c4[p, d].wait_recv()
        spot = rows(core * half + p * third + pos[p] * q1, q1)
        for d in steps:
            c5[p, d] = remote(full2.at[p], out_ref.at[spot], send5.at[p, d - 1], recv5.at[p, d - 1], along(p, d))
            c5[p, d].start()
        c6[p, 0] = remote(full2.at[p], out_ref.at[spot], send6.at[p, 0], recv6.at[p, 0], mate)
        c6[p, 0].start()
        own.append(pltpu.make_async_copy(full2.at[p], out_ref.at[spot], own_sem.at[p]))
        own[-1].start()
    for d in (1, 3, 2):
        for p in range(PARTS):
            c5[p, d].wait_recv()
            spot = rows(core * half + p * third + lax.rem(pos[p] + RING - d, RING) * q1, q1)
            c6[p, d] = remote(out_ref.at[spot], out_ref.at[spot], send6.at[p, d], recv6.at[p, d], mate)
            c6[p, d].start()
    for copies in (c0, c1, c2, c3, c4, c5, c6, c7):
        for copy in copies.values():
            copy.wait_send()
    for copy in own:
        copy.wait()
    for copies in (c6, c7):
        for copy in copies.values():
            copy.wait_recv()


def summed_gram(train, targets):
    rows, width = train.shape
    total_rows = len(upper_blocks(width // NB)) * NB
    third = total_rows // (2 * PARTS)
    q1, q2 = third // RING, third // (RING * RING)
    sem = pltpu.SemaphoreType.DMA
    fan = RING - 1
    pairs = [(PARTS,)] + [(PARTS, fan)] * 5 + [(PARTS, RING), (VISITS - 1,)]
    return pl.pallas_call(
        sum_kernel,
        out_shape=(
            jax.ShapeDtypeStruct((total_rows, NB), F32),
            jax.ShapeDtypeStruct((VISITS * targets.shape[0], targets.shape[1]), BF16),
        ),
        in_specs=[pl.BlockSpec(memory_space=pl.ANY)] * 2,
        out_specs=[pl.BlockSpec(memory_space=pl.ANY)] * 2,
        scratch_shapes=[
            pltpu.VMEM((rows, width), BF16),
            pltpu.VMEM((total_rows, NB), F32),
            pltpu.VMEM((PARTS, third, NB), F32),
            pltpu.VMEM((PARTS, third, NB), F32),
            pltpu.VMEM((PARTS, fan, q1, NB), F32),
            pltpu.VMEM((PARTS, q1, NB), F32),
            pltpu.VMEM((PARTS, fan, q2, NB), F32),
            pltpu.VMEM((PARTS, q2, NB), F32),
            pltpu.VMEM((PARTS, fan, q2, NB), F32),
            pltpu.VMEM((PARTS, q1, NB), F32),
        ]
        + [sem(shape) for shape in pairs for _ in range(2)]
        + [sem((PARTS + 1,)), sem((4,))],
        compiler_params=pltpu.CompilerParams(
            collective_id=0, has_side_effects=True, vmem_limit_bytes=56 << 20
        ),
        name="summed_gram",
    )(train, targets)


def per_device(train_grads, targets):
    rows_total = train_grads.shape[0] * lax.axis_size("grp") * lax.axis_size("blk")
    gram, right = summed_gram(train_grads, targets)
    return solve_and_score(gram, right, train_grads, rows_total)


def solution(mesh):
    spec = P(("grp", "blk"), None)
    return jax.shard_map(per_device, mesh=mesh, in_specs=(spec, spec), out_specs=spec, check_vma=False)
```

```python
import functools

import jax
import jax.numpy as jnp
from jax import lax
from jax.experimental import pallas as pl
from jax.experimental.pallas import tpu as pltpu
from jax.sharding import PartitionSpec as P

VISITS = 3
NB = 128
TILE = 256
F32 = jnp.float32
BF16 = jnp.bfloat16
MESH = pl.DeviceIdType.MESH


def panels(count):
    wide_count = count // 2
    order = [n for n in range(wide_count)]
    return [[order[-1], order[0]], order[1:-1][::-1]]


def upper_blocks(count):
    return [
        (i, c) for half in panels(count) for panel in half for c in (2 * panel, 2 * panel + 1) for i in range(c + 1)
    ]


def wide(x):
    return jnp.broadcast_to(x, (8, NB))


def split2(x):
    hi = x.astype(BF16)
    return hi, (x - hi.astype(F32)).astype(BF16)


def split3(x):
    hi = x.astype(BF16)
    rest = x - hi.astype(F32)
    mid = rest.astype(BF16)
    return hi, mid, (rest - mid.astype(F32)).astype(BF16)


def dot(a, b):
    return jnp.dot(a, b, preferred_element_type=F32)


def dot3(a, b):
    ah, al = a
    bh, bl = b
    return dot(jnp.concatenate([ah, al], axis=1), jnp.concatenate([bh, bh], axis=0)) + dot(ah, bl)


PAIRS = ((0, 0), (0, 1), (1, 0), (1, 1), (0, 2), (2, 0))


def dot6(a, b):
    left = jnp.concatenate([a[p] for p, _ in PAIRS], axis=1)
    return dot(left, jnp.concatenate([b[q] for _, q in PAIRS], axis=0))


def outer6(a, b):
    a, b = split3(a), split3(b)
    left = jnp.concatenate([a[p] for p, _ in PAIRS], axis=0)
    right = jnp.concatenate([b[q] for _, q in PAIRS], axis=0)
    return lax.dot_general(left, right, (((0,), (0,)), ((), ())), preferred_element_type=F32)


def total(terms):
    while len(terms) > 1:
        terms = [terms[i] + terms[i + 1] for i in range(0, len(terms), 2)]
    return terms[0]


def pivot_rows(rows, k, buf):
    lane = lax.broadcasted_iota(jnp.int32, (8, NB), 1)
    sub = lax.broadcasted_iota(jnp.int32, (8, NB), 0)
    y = jnp.where((lane >= k) & (lane < k + 8), -(lane == sub + k).astype(F32), rows)
    for j in range(8):
        buf[j] = wide(rows[:, k + j : k + j + 1])
    m = [buf[j] for j in range(8)]
    for b in range(0, 8, 2):
        if b == 0:
            row = lambda i, j: wide(buf[j, i : i + 1, :])
        else:
            row = lambda i, j: wide(m[j][i : i + 1, :])
        e, f, g = row(b, b), row(b, b + 1), row(b + 1, b + 1)
        inv = 1.0 / (e * g - f * f)
        ie, jf, ig = g * inv, f * inv, e * inv
        left0 = jnp.where(sub == b, -1.0, jnp.where(sub == b + 1, 0.0, m[b]))
        left1 = jnp.where(sub == b + 1, -1.0, jnp.where(sub == b, 0.0, m[b + 1]))
        pair = (sub == b) | (sub == b + 1)

        def step(x, x0, x1):
            u0, u1 = ie * x0 - jf * x1, ig * x1 - jf * x0
            return jnp.where(pair, 0.0, x) - (left0 * u0 + left1 * u1)

        for j in range(b + 2, 8):
            m[j] = step(m[j], row(b, j), row(b + 1, j))
        y = step(y, wide(y[b : b + 1, :]), wide(y[b + 1 : b + 2, :]))
    return y


def neg_inverse(a, buf, beside=()):
    lane = lax.broadcasted_iota(jnp.int32, (8, NB), 1)
    a = list(a)
    count = len(a)
    for g in range(count):
        k = 8 * g
        own = (lane >= k) & (lane < k + 8)
        rows = a[g]
        y = pivot_rows(rows, k, buf.at[g % 2])
        if g + 1 < count:
            t = a[g + 1]
            terms = [wide(t[:, k + j : k + j + 1]) * wide(y[j : j + 1, :]) for j in range(8)]
            a[g + 1] = jnp.where(own, 0.0, t) - total(terms)
        change = outer6(rows, y)
        for call in beside[g * len(beside) // count : (g + 1) * len(beside) // count]:
            call()
        for t in range(count):
            if t != g and t != g + 1:
                a[t] = jnp.where(own, 0.0, a[t]) - change[8 * t : 8 * t + 8, :]
        a[g] = y
    return a


def inverse(block, buf, beside=()):
    block = 0.5 * (block + block.T)
    tiles = [block[8 * t : 8 * t + 8, :] for t in range(NB // 8)]
    return -jnp.concatenate(neg_inverse(tiles, buf, beside), axis=0)


def solve_kernel(
    rows_total, gram_ref, right_ref, train_ref, out_ref, mat, left, right, panel, pivot, buf, held, scored, x_ref, in_sem, out_sem
):
    width = right_ref.shape[1]
    nblk = width // NB
    nrhs = right_ref.shape[0]
    rows = train_ref.shape[0]
    pieces = 8
    depth = rows // pieces
    load = pltpu.make_async_copy(train_ref, held, in_sem)
    load.start()

    eye = (lax.broadcasted_iota(jnp.int32, (NB, NB), 0) == lax.broadcasted_iota(jnp.int32, (NB, NB), 1)).astype(F32)
    blocks = upper_blocks(nblk)
    diag = jnp.zeros((NB, NB), F32)
    for n, (i, c) in enumerate(blocks):
        if i == c:
            diag = diag + gram_ref[n * NB : (n + 1) * NB, :] * eye
    trace = jnp.sum(jnp.sum(diag, axis=0, keepdims=True), axis=1, keepdims=True)
    damping = (0.1 * trace) / (rows_total * width)
    for n, (i, c) in enumerate(blocks):
        block = gram_ref[n * NB : (n + 1) * NB, :] * (1.0 / rows_total)
        if i == c:
            mat[i * NB : (i + 1) * NB, i * NB : (i + 1) * NB] = block + damping * eye
        else:
            mat[i * NB : (i + 1) * NB, c * NB : (c + 1) * NB] = block
            mat[c * NB : (c + 1) * NB, i * NB : (i + 1) * NB] = block.T
    for c in range(nrhs // NB):
        mat[:, width + c * NB : width + (c + 1) * NB] = right_ref[c * NB : (c + 1) * NB, :].astype(F32).T

    def pivot_row(j, start):
        here = pl.ds(j * NB if isinstance(j, int) else pl.multiple_of(j * NB, NB), NB)
        inv = split3(pivot[...])
        inv = jnp.concatenate([inv[p] for p, _ in PAIRS], axis=1)
        for c in range(start, width + nrhs, TILE):
            cols = slice(c, min(c + TILE, width + nrhs))
            row = split3(mat[here, cols])
            w = dot(inv, jnp.concatenate([row[q] for _, q in PAIRS], axis=0))
            wh, wl = split2(w)
            for n, part in enumerate((wh, wh, wl)):
                right[n * NB : (n + 1) * NB, cols] = part
            panel[:, cols] = w
        hi, lo = split2(mat[:, here])
        left[:, :NB] = hi
        left[:, NB : 2 * NB] = lo
        left[:, 2 * NB :] = hi
        return here

    def update(r, c):
        def call():
            some, cols = slice(r, r + TILE), slice(c, min(c + TILE, width + nrhs))
            mat[some, cols] -= dot(left[some, :], right[:, cols])

        return call

    def step(j, _):
        here = pivot_row(j, NB)
        there = pl.ds(pl.multiple_of(j * NB + NB, NB), NB)
        ahead = mat[there, there] - dot(left[there, :], right[:, there])
        calls = [update(r, c) for c in range(NB, width + nrhs, TILE) for r in range(0, width, TILE)]
        pivot[...] = inverse(ahead, buf, calls)
        mat[here, NB:] = panel[:, NB:]
        return 0

    pivot[...] = inverse(mat[:NB, :NB], buf)
    lax.fori_loop(0, nblk - 1, step, 0)
    here = pivot_row(nblk - 1, width)
    for c in range(width, width + nrhs, TILE):
        for r in range(0, width, TILE):
            update(r, c)()
    mat[here, width:] = panel[:, width:]
    x_ref[...] = mat[:, width:].astype(BF16)
    load.wait()
    scale = 1.0 / (width ** 0.5)

    def score(p, _):
        part = pl.ds(pl.multiple_of(p * depth, depth), depth)
        scored[part, :] = (dot(held[part, :], x_ref[...]) * scale).astype(BF16)
        pltpu.make_async_copy(scored.at[part], out_ref.at[part], out_sem).start()
        return 0

    lax.fori_loop(0, pieces, score, 0)
    pltpu.make_async_copy(scored, out_ref, out_sem).wait()


def solve_and_score(gram, right, train, rows_total):
    rows, width = train.shape
    nrhs = right.shape[0]
    return pl.pallas_call(
        functools.partial(solve_kernel, rows_total),
        out_shape=jax.ShapeDtypeStruct((rows, nrhs), BF16),
        in_specs=[
            pl.BlockSpec(memory_space=pltpu.VMEM),
            pl.BlockSpec(memory_space=pltpu.VMEM),
            pl.BlockSpec(memory_space=pl.ANY),
        ],
        out_specs=pl.BlockSpec(memory_space=pl.ANY),
        scratch_shapes=[
            pltpu.VMEM((width, width + nrhs), F32),
            pltpu.VMEM((width, 3 * NB), BF16),
            pltpu.VMEM((3 * NB, width + nrhs), BF16),
            pltpu.VMEM((NB, width + nrhs), F32),
            pltpu.VMEM((NB, NB), F32),
            pltpu.VMEM((2, 8, 8, NB), F32),
            pltpu.VMEM((rows, width), BF16),
            pltpu.VMEM((rows, nrhs), BF16),
            pltpu.VMEM((width, nrhs), BF16),
            pltpu.SemaphoreType.DMA,
            pltpu.SemaphoreType.DMA,
        ],
        compiler_params=pltpu.CompilerParams(vmem_limit_bytes=56 << 20),
        name="solve_and_score",
    )(gram, right, train)


RING = 4
PARTS = 3


def gram_panel(panel, known, held, turned, gram, loads, place):
    rows = held.shape[0]
    depth = rows // len(loads)
    last = (panel + 1) * 2 * NB
    for k, load in enumerate(loads):
        if load is not None:
            load.wait()
        some = slice(k * depth, (k + 1) * depth)
        if known < last:
            turned[known:last, some] = held[some, known:last].T
        res = dot(turned[:last, some], held[some, panel * 2 * NB : last])
        for n in range(2):
            c = 2 * panel + n
            for i in range(c + 1):
                spot = slice(place[i, c] * NB, place[i, c] * NB + NB)
                block = res[i * NB : (i + 1) * NB, n * NB : (n + 1) * NB]
                if k == 0:
                    gram[spot, :] = block
                else:
                    gram[spot, :] += block
    return max(known, last)


def sum_kernel(
    train_ref, target_ref, out_ref, right_ref, held, turned, gram_ref, pair, work, got1, sum1, got2, sum2, got3, full2,
    send0, recv0, send1, recv1, send2, recv2, send3, recv3, send4, recv4, send5, recv5, send6, recv6, send7, recv7,
    own_sem, load_sem,
):
    chunks = load_sem.shape[0]
    depth = held.shape[0] // chunks
    loads = [
        pltpu.make_async_copy(train_ref.at[pl.ds(k * depth, depth)], held.at[pl.ds(k * depth, depth)], load_sem.at[k])
        for k in range(chunks)
    ]
    for load in loads:
        load.start()
    nblk = held.shape[1] // NB
    halves = panels(nblk)
    place = {key: n for n, key in enumerate(upper_blocks(nblk))}
    grp, blk = lax.axis_index("grp"), lax.axis_index("blk")
    core = lax.rem(grp, 2)
    pos = (lax.rem(blk, 2) * 2 + grp // 2, blk // 8, lax.rem(blk // 2, RING))

    def device(where, which):
        x, y, z = where
        return (lax.rem(x, 2) * 2 + which, (y * RING + z) * 2 + x // 2)

    def along(axis, d):
        where = list(pos)
        where[axis] = lax.rem(where[axis] + d, RING)
        return device(where, core)

    mate = device(pos, 1 - core)
    blks = lax.axis_size("blk")
    ahead = [(grp, lax.rem(blk + s, blks)) for s in range(1, VISITS)]
    behind = [(grp, lax.rem(blk + blks - s, blks)) for s in range(1, VISITS)]
    mates = [mate] + [along(axis, d) for axis in range(3) for d in range(1, RING)]

    barrier = pltpu.get_barrier_semaphore()
    for other in mates + behind:
        pl.semaphore_signal(barrier, inc=1, device_id=other, device_id_type=MESH)

    done = [None] * chunks
    for c in range(2):

        @pl.when(core == c)
        def _():
            known = 0
            for n, panel in enumerate(halves[1 - c]):
                known = gram_panel(panel, known, held, turned, gram_ref, done if n else loads, place)

    pl.semaphore_wait(barrier, len(mates) + len(ahead))

    def remote(src, dst, send, recv, who):
        return pltpu.make_async_remote_copy(
            src_ref=src, dst_ref=dst, send_sem=send, recv_sem=recv, device_id=who, device_id_type=MESH
        )

    half = gram_ref.shape[0] // 2
    third = half // PARTS
    q1 = third // RING
    q2 = q1 // RING

    def rows(start, size):
        return pl.ds(pl.multiple_of(start, 8), size)

    c0, c1, c2, c3, c4, c5, c6, c7 = {}, {}, {}, {}, {}, {}, {}, {}
    for p in range(PARTS):
        c0[p] = remote(
            gram_ref.at[rows((1 - core) * half + p * third, third)], pair.at[p], send0.at[p], recv0.at[p], mate
        )
        c0[p].start()
    nt = target_ref.shape[0]
    for s in range(1, VISITS):
        c7[s] = remote(target_ref, right_ref.at[pl.ds(s * nt, nt)], send7.at[s - 1], recv7.at[s - 1], ahead[s - 1])
        c7[s].start()
    own = [pltpu.make_async_copy(target_ref, right_ref.at[pl.ds(0, nt)], own_sem.at[PARTS])]
    own[0].start()
    for c in range(2):

        @pl.when(core == c)
        def _():
            known = 2 * NB * (max(halves[1 - c]) + 1)
            for panel in halves[c]:
                known = gram_panel(panel, known, held, turned, gram_ref, done, place)

    steps = range(1, RING)
    for p in range(PARTS):
        axis = p
        c0[p].wait_recv()
        work[p] = gram_ref[rows(core * half + p * third, third), :] + pair[p]
        for d in steps:
            c1[p, d] = remote(
                work.at[p, rows(lax.rem(pos[axis] + d, RING) * q1, q1)],
                got1.at[p, d - 1], send1.at[p, d - 1], recv1.at[p, d - 1], along(axis, d),
            )
            c1[p, d].start()
    for p in range(PARTS):
        axis = (p + 1) % 3
        for d in steps:
            c1[p, d].wait_recv()
        mine = work[p, rows(pos[p] * q1, q1), :]
        sum1[p] = (mine + got1[p, 0]) + (got1[p, 1] + got1[p, 2])
        for d in steps:
            c2[p, d] = remote(
                sum1.at[p, rows(lax.rem(pos[axis] + d, RING) * q2, q2)],
                got2.at[p, d - 1], send2.at[p, d - 1], recv2.at[p, d - 1], along(axis, d),
            )
            c2[p, d].start()
    for p in range(PARTS):
        axis = (p + 2) % 3
        for d in steps:
            c2[p, d].wait_recv()
        mine = sum1[p, rows(pos[(p + 1) % 3] * q2, q2), :]
        sum2[p] = (mine + got2[p, 0]) + (got2[p, 1] + got2[p, 2])
        for d in steps:
            c3[p, d] = remote(sum2.at[p], got3.at[p, d - 1], send3.at[p, d - 1], recv3.at[p, d - 1], along(axis, d))
            c3[p, d].start()
    for p in range(PARTS):
        axis = (p + 1) % 3
        for d in steps:
            c3[p, d].wait_recv()
        spot = rows(pos[axis] * q2, q2)
        full2[p, spot, :] = (sum2[p] + got3[p, 0]) + (got3[p, 1] + got3[p, 2])
        for d in steps:
            c4[p, d] = remote(
                full2.at[p, spot], full2.at[p, spot], send4.at[p, d - 1], recv4.at[p, d - 1], along(axis, d)
            )
            c4[p, d].start()
    for p in range(PARTS):
        for d in steps:
            c4[p, d].wait_recv()
        spot = rows(core * half + p * third + pos[p] * q1, q1)
        for d in steps:
            c5[p, d] = remote(full2.at[p], out_ref.at[spot], send5.at[p, d - 1], recv5.at[p, d - 1], along(p, d))
            c5[p, d].start()
        c6[p, 0] = remote(full2.at[p], out_ref.at[spot], send6.at[p, 0], recv6.at[p, 0], mate)
        c6[p, 0].start()
        own.append(pltpu.make_async_copy(full2.at[p], out_ref.at[spot], own_sem.at[p]))
        own[-1].start()
    for d in (1, 3, 2):
        for p in range(PARTS):
            c5[p, d].wait_recv()
            spot = rows(core * half + p * third + lax.rem(pos[p] + RING - d, RING) * q1, q1)
            c6[p, d] = remote(out_ref.at[spot], out_ref.at[spot], send6.at[p, d], recv6.at[p, d], mate)
            c6[p, d].start()
    for copies in (c0, c1, c2, c3, c4, c5, c6, c7):
        for copy in copies.values():
            copy.wait_send()
    for copy in own:
        copy.wait()
    for copies in (c6, c7):
        for copy in copies.values():
            copy.wait_recv()


def summed_gram(train, targets):
    rows, width = train.shape
    total_rows = len(upper_blocks(width // NB)) * NB
    third = total_rows // (2 * PARTS)
    q1, q2 = third // RING, third // (RING * RING)
    sem = pltpu.SemaphoreType.DMA
    fan = RING - 1
    pairs = [(PARTS,)] + [(PARTS, fan)] * 5 + [(PARTS, RING), (VISITS - 1,)]
    return pl.pallas_call(
        sum_kernel,
        out_shape=(
            jax.ShapeDtypeStruct((total_rows, NB), F32),
            jax.ShapeDtypeStruct((VISITS * targets.shape[0], targets.shape[1]), BF16),
        ),
        in_specs=[pl.BlockSpec(memory_space=pl.ANY)] * 2,
        out_specs=[pl.BlockSpec(memory_space=pl.ANY)] * 2,
        scratch_shapes=[
            pltpu.VMEM((rows, width), BF16),
            pltpu.VMEM((width, rows), BF16),
            pltpu.VMEM((total_rows, NB), F32),
            pltpu.VMEM((PARTS, third, NB), F32),
            pltpu.VMEM((PARTS, third, NB), F32),
            pltpu.VMEM((PARTS, fan, q1, NB), F32),
            pltpu.VMEM((PARTS, q1, NB), F32),
            pltpu.VMEM((PARTS, fan, q2, NB), F32),
            pltpu.VMEM((PARTS, q2, NB), F32),
            pltpu.VMEM((PARTS, fan, q2, NB), F32),
            pltpu.VMEM((PARTS, q1, NB), F32),
        ]
        + [sem(shape) for shape in pairs for _ in range(2)]
        + [sem((PARTS + 1,)), sem((4,))],
        compiler_params=pltpu.CompilerParams(
            collective_id=0, has_side_effects=True, vmem_limit_bytes=56 << 20
        ),
        name="summed_gram",
    )(train, targets)


def per_device(train_grads, targets):
    rows_total = train_grads.shape[0] * lax.axis_size("grp") * lax.axis_size("blk")
    gram, right = summed_gram(train_grads, targets)
    return solve_and_score(gram, right, train_grads, rows_total)


def solution(mesh):
    spec = P(("grp", "blk"), None)
    return jax.shard_map(per_device, mesh=mesh, in_specs=(spec, spec), out_specs=spec, check_vma=False)
```

```python
import functools

import jax
import jax.numpy as jnp
from jax import lax
from jax.experimental import pallas as pl
from jax.experimental.pallas import tpu as pltpu
from jax.sharding import PartitionSpec as P

VISITS = 3
NB = 128
TILE = 256
NEAR = 1
STAGES = ((0, 7),)
ROWS = 128
F32 = jnp.float32
BF16 = jnp.bfloat16
MESH = pl.DeviceIdType.MESH


def panels(count):
    wide_count = count // 2
    order = [n for n in range(wide_count)]
    return [[order[-1], order[0]], order[1:-1][::-1]]


def upper_blocks(count):
    return [
        (i, c) for half in panels(count) for panel in half for c in (2 * panel, 2 * panel + 1) for i in range(c + 1)
    ]


def wide(x):
    return jnp.broadcast_to(x, (8, NB))


def split2(x):
    hi = x.astype(BF16)
    return hi, (x - hi.astype(F32)).astype(BF16)


def split3(x):
    hi = x.astype(BF16)
    rest = x - hi.astype(F32)
    mid = rest.astype(BF16)
    return hi, mid, (rest - mid.astype(F32)).astype(BF16)


def dot(a, b):
    return jnp.dot(a, b, preferred_element_type=F32)


def dot3(a, b):
    ah, al = a
    bh, bl = b
    return dot(jnp.concatenate([ah, al], axis=1), jnp.concatenate([bh, bh], axis=0)) + dot(ah, bl)


PAIRS = ((0, 0), (0, 1), (1, 0), (1, 1), (0, 2), (2, 0))


def dot6(a, b):
    left = jnp.concatenate([a[p] for p, _ in PAIRS], axis=1)
    return dot(left, jnp.concatenate([b[q] for _, q in PAIRS], axis=0))


def outer6(a, b):
    a, b = split3(a), split3(b)
    left = jnp.concatenate([a[p] for p, _ in PAIRS], axis=0)
    right = jnp.concatenate([b[q] for _, q in PAIRS], axis=0)
    return lax.dot_general(left, right, (((0,), (0,)), ((), ())), preferred_element_type=F32)


def total(terms):
    while len(terms) > 1:
        terms = [terms[i] + terms[i + 1] for i in range(0, len(terms), 2)]
    return terms[0]


def pivot_rows(rows, k, buf):
    lane = lax.broadcasted_iota(jnp.int32, (8, NB), 1)
    sub = lax.broadcasted_iota(jnp.int32, (8, NB), 0)
    y = jnp.where((lane >= k) & (lane < k + 8), -(lane == sub + k).astype(F32), rows)
    for j in range(8):
        buf[j] = wide(rows[:, k + j : k + j + 1])
    m = [buf[j] for j in range(8)]
    for b in range(0, 8, 2):
        if b == 0:
            row = lambda i, j: wide(buf[j, i : i + 1, :])
        else:
            row = lambda i, j: wide(m[j][i : i + 1, :])
        e, f, g = row(b, b), row(b, b + 1), row(b + 1, b + 1)
        inv = 1.0 / (e * g - f * f)
        ie, jf, ig = g * inv, f * inv, e * inv
        left0 = jnp.where(sub == b, -1.0, jnp.where(sub == b + 1, 0.0, m[b]))
        left1 = jnp.where(sub == b + 1, -1.0, jnp.where(sub == b, 0.0, m[b + 1]))
        pair = (sub == b) | (sub == b + 1)

        def step(x, x0, x1):
            u0, u1 = ie * x0 - jf * x1, ig * x1 - jf * x0
            return jnp.where(pair, 0.0, x) - (left0 * u0 + left1 * u1)

        for j in range(b + 2, 8):
            m[j] = step(m[j], row(b, j), row(b + 1, j))
        y = step(y, wide(y[b : b + 1, :]), wide(y[b + 1 : b + 2, :]))
    return y


def neg_inverse(a, buf, beside=()):
    lane = lax.broadcasted_iota(jnp.int32, (8, NB), 1)
    a = list(a)
    count = len(a)
    for g in range(count):
        k = 8 * g
        own = (lane >= k) & (lane < k + 8)
        rows = a[g]
        y = pivot_rows(rows, k, buf.at[g % 2])
        near = range(g + 1, min(g + 1 + NEAR, count))
        for n in near:
            terms = [wide(a[n][:, k + j : k + j + 1]) * wide(y[j : j + 1, :]) for j in range(8)]
            a[n] = jnp.where(own, 0.0, a[n]) - total(terms)
        for call in beside[g * len(beside) // count : (g + 1) * len(beside) // count]:
            call()
        change = outer6(rows, y)
        for t in range(count):
            if t != g and t not in near:
                a[t] = jnp.where(own, 0.0, a[t]) - change[8 * t : 8 * t + 8, :]
        a[g] = y
    return a


def inverse(block, buf, beside=()):
    block = 0.5 * (block + block.T)
    tiles = [block[8 * t : 8 * t + 8, :] for t in range(NB // 8)]
    return -jnp.concatenate(neg_inverse(tiles, buf, beside), axis=0)


def solve_kernel(
    rows_total, gram_ref, right_ref, train_ref, out_ref, mat, left, right, panel, pivot, buf, held, scored, x_ref, in_sem, out_sem
):
    width = right_ref.shape[1]
    nblk = width // NB
    nrhs = right_ref.shape[0]
    rows = train_ref.shape[0]
    pieces = 8
    depth = rows // pieces
    load = pltpu.make_async_copy(train_ref, held, in_sem)
    load.start()

    eye = (lax.broadcasted_iota(jnp.int32, (NB, NB), 0) == lax.broadcasted_iota(jnp.int32, (NB, NB), 1)).astype(F32)
    blocks = upper_blocks(nblk)
    diag = jnp.zeros((NB, NB), F32)
    for n, (i, c) in enumerate(blocks):
        if i == c:
            diag = diag + gram_ref[n * NB : (n + 1) * NB, :] * eye
    trace = jnp.sum(jnp.sum(diag, axis=0, keepdims=True), axis=1, keepdims=True)
    damping = (0.1 * trace) / (rows_total * width)
    for n, (i, c) in enumerate(blocks):
        block = gram_ref[n * NB : (n + 1) * NB, :] * (1.0 / rows_total)
        if i == c:
            mat[i * NB : (i + 1) * NB, i * NB : (i + 1) * NB] = block + damping * eye
        else:
            mat[i * NB : (i + 1) * NB, c * NB : (c + 1) * NB] = block
            mat[c * NB : (c + 1) * NB, i * NB : (i + 1) * NB] = block.T
    for c in range(nrhs // NB):
        mat[:, width + c * NB : width + (c + 1) * NB] = right_ref[c * NB : (c + 1) * NB, :].astype(F32).T

    def rows_of(j):
        return pl.ds(j * NB if isinstance(j, int) else pl.multiple_of(j * NB, NB), NB)

    def pivot_row(here, inv, c):
        def call():
            cols = slice(c, min(c + TILE, width + nrhs))
            row = split3(mat[here, cols])
            w = dot(inv, jnp.concatenate([row[q] for _, q in PAIRS], axis=0))
            wh, wl = split2(w)
            for n, part in enumerate((wh, wh, wl)):
                right[n * NB : (n + 1) * NB, cols] = part
            panel[:, cols] = w

        return call

    def pivot_column(here, some):
        hi, lo = split2(mat[some, here])
        left[some, :NB] = hi
        left[some, NB : 2 * NB] = lo
        left[some, 2 * NB :] = hi

    def update(r, c):
        def call():
            some, cols = slice(r, r + ROWS), slice(c, min(c + TILE, width + nrhs))
            mat[some, cols] -= dot(left[some, :], right[:, cols])

        return call

    def stacked_inverse():
        inv = split3(pivot[...])
        return jnp.concatenate([inv[p] for p, _ in PAIRS], axis=1)

    def step(start, j, _):
        here, there = rows_of(j), rows_of(j + 1)
        inv = stacked_inverse()
        w = dot(inv, jnp.concatenate([split3(mat[here, there])[q] for _, q in PAIRS], axis=0))
        wh, wl = split2(w)
        hi, lo = split2(mat[there, here])
        ahead = mat[there, there] - dot(
            jnp.concatenate([hi, lo, hi], axis=1), jnp.concatenate([wh, wh, wl], axis=0)
        )
        pivot_column(here, slice(0, width))
        calls = []
        for c in range(start, width + nrhs, TILE):
            pivot_row(here, inv, c)()
            calls += [update(r, c) for r in range(0, width, ROWS)]
        pivot[...] = inverse(ahead, buf, calls)
        mat[here, start:] = panel[:, start:]
        return 0

    pivot[...] = inverse(mat[:NB, :NB], buf)
    for first, last in STAGES:
        lax.fori_loop(first, last, functools.partial(step, (first + 1) * NB), 0)
    here = rows_of(nblk - 1)
    pivot_column(here, slice(0, width))
    for c in range(width, width + nrhs, TILE):
        pivot_row(here, stacked_inverse(), c)()
        for r in range(0, width, ROWS):
            update(r, c)()
    mat[here, width:] = panel[:, width:]
    x_ref[...] = mat[:, width:].astype(BF16)
    load.wait()
    scale = 1.0 / (width ** 0.5)

    def score(p, _):
        part = pl.ds(pl.multiple_of(p * depth, depth), depth)
        scored[part, :] = (dot(held[part, :], x_ref[...]) * scale).astype(BF16)
        pltpu.make_async_copy(scored.at[part], out_ref.at[part], out_sem).start()
        return 0

    lax.fori_loop(0, pieces, score, 0)
    pltpu.make_async_copy(scored, out_ref, out_sem).wait()


def solve_and_score(gram, right, train, rows_total):
    rows, width = train.shape
    nrhs = right.shape[0]
    return pl.pallas_call(
        functools.partial(solve_kernel, rows_total),
        out_shape=jax.ShapeDtypeStruct((rows, nrhs), BF16),
        in_specs=[
            pl.BlockSpec(memory_space=pltpu.VMEM),
            pl.BlockSpec(memory_space=pltpu.VMEM),
            pl.BlockSpec(memory_space=pl.ANY),
        ],
        out_specs=pl.BlockSpec(memory_space=pl.ANY),
        scratch_shapes=[
            pltpu.VMEM((width, width + nrhs), F32),
            pltpu.VMEM((width, 3 * NB), BF16),
            pltpu.VMEM((3 * NB, width + nrhs), BF16),
            pltpu.VMEM((NB, width + nrhs), F32),
            pltpu.VMEM((NB, NB), F32),
            pltpu.VMEM((2, 8, 8, NB), F32),
            pltpu.VMEM((rows, width), BF16),
            pltpu.VMEM((rows, nrhs), BF16),
            pltpu.VMEM((width, nrhs), BF16),
            pltpu.SemaphoreType.DMA,
            pltpu.SemaphoreType.DMA,
        ],
        compiler_params=pltpu.CompilerParams(vmem_limit_bytes=56 << 20),
        name="solve_and_score",
    )(gram, right, train)


RING = 4
PARTS = 3


def gram_panel(panel, known, held, turned, gram, loads, place):
    rows = held.shape[0]
    depth = rows // len(loads)
    last = (panel + 1) * 2 * NB
    for k, load in enumerate(loads):
        if load is not None:
            load.wait()
        some = slice(k * depth, (k + 1) * depth)
        if known < last:
            turned[known:last, some] = held[some, known:last].T
        res = dot(turned[:last, some], held[some, panel * 2 * NB : last])
        for n in range(2):
            c = 2 * panel + n
            for i in range(c + 1):
                spot = slice(place[i, c] * NB, place[i, c] * NB + NB)
                block = res[i * NB : (i + 1) * NB, n * NB : (n + 1) * NB]
                if k == 0:
                    gram[spot, :] = block
                else:
                    gram[spot, :] += block
    return max(known, last)


def sum_kernel(
    train_ref, target_ref, out_ref, right_ref, held, turned, gram_ref, pair, work, got1, sum1, got2, sum2, got3, full2,
    send0, recv0, send1, recv1, send2, recv2, send3, recv3, send4, recv4, send5, recv5, send6, recv6, send7, recv7,
    own_sem, load_sem,
):
    chunks = load_sem.shape[0]
    depth = held.shape[0] // chunks
    loads = [
        pltpu.make_async_copy(train_ref.at[pl.ds(k * depth, depth)], held.at[pl.ds(k * depth, depth)], load_sem.at[k])
        for k in range(chunks)
    ]
    for load in loads:
        load.start()
    nblk = held.shape[1] // NB
    halves = panels(nblk)
    place = {key: n for n, key in enumerate(upper_blocks(nblk))}
    grp, blk = lax.axis_index("grp"), lax.axis_index("blk")
    core = lax.rem(grp, 2)
    pos = (lax.rem(blk, 2) * 2 + grp // 2, blk // 8, lax.rem(blk // 2, RING))

    def device(where, which):
        x, y, z = where
        return (lax.rem(x, 2) * 2 + which, (y * RING + z) * 2 + x // 2)

    def along(axis, d):
        where = list(pos)
        where[axis] = lax.rem(where[axis] + d, RING)
        return device(where, core)

    mate = device(pos, 1 - core)
    blks = lax.axis_size("blk")
    ahead = [(grp, lax.rem(blk + s, blks)) for s in range(1, VISITS)]
    behind = [(grp, lax.rem(blk + blks - s, blks)) for s in range(1, VISITS)]
    mates = [mate] + [along(axis, d) for axis in range(3) for d in range(1, RING)]

    barrier = pltpu.get_barrier_semaphore()
    for other in mates + behind:
        pl.semaphore_signal(barrier, inc=1, device_id=other, device_id_type=MESH)

    done = [None] * chunks
    for c in range(2):

        @pl.when(core == c)
        def _():
            known = 0
            for n, panel in enumerate(halves[1 - c]):
                known = gram_panel(panel, known, held, turned, gram_ref, done if n else loads, place)

    pl.semaphore_wait(barrier, len(mates) + len(ahead))

    def remote(src, dst, send, recv, who):
        return pltpu.make_async_remote_copy(
            src_ref=src, dst_ref=dst, send_sem=send, recv_sem=recv, device_id=who, device_id_type=MESH
        )

    half = gram_ref.shape[0] // 2
    third = half // PARTS
    q1 = third // RING
    q2 = q1 // RING

    def rows(start, size):
        return pl.ds(pl.multiple_of(start, 8), size)

    c0, c1, c2, c3, c4, c5, c6, c7 = {}, {}, {}, {}, {}, {}, {}, {}
    for p in range(PARTS):
        c0[p] = remote(
            gram_ref.at[rows((1 - core) * half + p * third, third)], pair.at[p], send0.at[p], recv0.at[p], mate
        )
        c0[p].start()
    nt = target_ref.shape[0]
    for s in range(1, VISITS):
        c7[s] = remote(target_ref, right_ref.at[pl.ds(s * nt, nt)], send7.at[s - 1], recv7.at[s - 1], ahead[s - 1])
        c7[s].start()
    own = [pltpu.make_async_copy(target_ref, right_ref.at[pl.ds(0, nt)], own_sem.at[PARTS])]
    own[0].start()
    for c in range(2):

        @pl.when(core == c)
        def _():
            known = 2 * NB * (max(halves[1 - c]) + 1)
            for panel in halves[c]:
                known = gram_panel(panel, known, held, turned, gram_ref, done, place)

    steps = range(1, RING)
    for p in range(PARTS):
        axis = p
        c0[p].wait_recv()
        work[p] = gram_ref[rows(core * half + p * third, third), :] + pair[p]
        for d in steps:
            c1[p, d] = remote(
                work.at[p, rows(lax.rem(pos[axis] + d, RING) * q1, q1)],
                got1.at[p, d - 1], send1.at[p, d - 1], recv1.at[p, d - 1], along(axis, d),
            )
            c1[p, d].start()
    for p in range(PARTS):
        axis = (p + 1) % 3
        for d in steps:
            c1[p, d].wait_recv()
        mine = work[p, rows(pos[p] * q1, q1), :]
        sum1[p] = (mine + got1[p, 0]) + (got1[p, 1] + got1[p, 2])
        for d in steps:
            c2[p, d] = remote(
                sum1.at[p, rows(lax.rem(pos[axis] + d, RING) * q2, q2)],
                got2.at[p, d - 1], send2.at[p, d - 1], recv2.at[p, d - 1], along(axis, d),
            )
            c2[p, d].start()
    for p in range(PARTS):
        axis = (p + 2) % 3
        for d in steps:
            c2[p, d].wait_recv()
        mine = sum1[p, rows(pos[(p + 1) % 3] * q2, q2), :]
        sum2[p] = (mine + got2[p, 0]) + (got2[p, 1] + got2[p, 2])
        for d in steps:
            c3[p, d] = remote(sum2.at[p], got3.at[p, d - 1], send3.at[p, d - 1], recv3.at[p, d - 1], along(axis, d))
            c3[p, d].start()
    for p in range(PARTS):
        axis = (p + 1) % 3
        for d in steps:
            c3[p, d].wait_recv()
        spot = rows(pos[axis] * q2, q2)
        full2[p, spot, :] = (sum2[p] + got3[p, 0]) + (got3[p, 1] + got3[p, 2])
        for d in steps:
            c4[p, d] = remote(
                full2.at[p, spot], full2.at[p, spot], send4.at[p, d - 1], recv4.at[p, d - 1], along(axis, d)
            )
            c4[p, d].start()
    for p in range(PARTS):
        for d in steps:
            c4[p, d].wait_recv()
        spot = rows(core * half + p * third + pos[p] * q1, q1)
        for d in steps:
            c5[p, d] = remote(full2.at[p], out_ref.at[spot], send5.at[p, d - 1], recv5.at[p, d - 1], along(p, d))
            c5[p, d].start()
        c6[p, 0] = remote(full2.at[p], out_ref.at[spot], send6.at[p, 0], recv6.at[p, 0], mate)
        c6[p, 0].start()
        own.append(pltpu.make_async_copy(full2.at[p], out_ref.at[spot], own_sem.at[p]))
        own[-1].start()
    for d in (1, 3, 2):
        for p in range(PARTS):
            c5[p, d].wait_recv()
            spot = rows(core * half + p * third + lax.rem(pos[p] + RING - d, RING) * q1, q1)
            c6[p, d] = remote(out_ref.at[spot], out_ref.at[spot], send6.at[p, d], recv6.at[p, d], mate)
            c6[p, d].start()
    for copies in (c0, c1, c2, c3, c4, c5, c6, c7):
        for copy in copies.values():
            copy.wait_send()
    for copy in own:
        copy.wait()
    for copies in (c6, c7):
        for copy in copies.values():
            copy.wait_recv()


def summed_gram(train, targets):
    rows, width = train.shape
    total_rows = len(upper_blocks(width // NB)) * NB
    third = total_rows // (2 * PARTS)
    q1, q2 = third // RING, third // (RING * RING)
    sem = pltpu.SemaphoreType.DMA
    fan = RING - 1
    pairs = [(PARTS,)] + [(PARTS, fan)] * 5 + [(PARTS, RING), (VISITS - 1,)]
    return pl.pallas_call(
        sum_kernel,
        out_shape=(
            jax.ShapeDtypeStruct((total_rows, NB), F32),
            jax.ShapeDtypeStruct((VISITS * targets.shape[0], targets.shape[1]), BF16),
        ),
        in_specs=[pl.BlockSpec(memory_space=pl.ANY)] * 2,
        out_specs=[pl.BlockSpec(memory_space=pl.ANY)] * 2,
        scratch_shapes=[
            pltpu.VMEM((rows, width), BF16),
            pltpu.VMEM((width, rows), BF16),
            pltpu.VMEM((total_rows, NB), F32),
            pltpu.VMEM((PARTS, third, NB), F32),
            pltpu.VMEM((PARTS, third, NB), F32),
            pltpu.VMEM((PARTS, fan, q1, NB), F32),
            pltpu.VMEM((PARTS, q1, NB), F32),
            pltpu.VMEM((PARTS, fan, q2, NB), F32),
            pltpu.VMEM((PARTS, q2, NB), F32),
            pltpu.VMEM((PARTS, fan, q2, NB), F32),
            pltpu.VMEM((PARTS, q1, NB), F32),
        ]
        + [sem(shape) for shape in pairs for _ in range(2)]
        + [sem((PARTS + 1,)), sem((4,))],
        compiler_params=pltpu.CompilerParams(
            collective_id=0, has_side_effects=True, vmem_limit_bytes=56 << 20
        ),
        name="summed_gram",
    )(train, targets)


def per_device(train_grads, targets):
    rows_total = train_grads.shape[0] * lax.axis_size("grp") * lax.axis_size("blk")
    gram, right = summed_gram(train_grads, targets)
    return solve_and_score(gram, right, train_grads, rows_total)


def solution(mesh):
    spec = P(("grp", "blk"), None)
    return jax.shard_map(per_device, mesh=mesh, in_specs=(spec, spec), out_specs=spec, check_vma=False)
```

```python
import functools

import jax
import jax.numpy as jnp
from jax import lax
from jax.experimental import pallas as pl
from jax.experimental.pallas import tpu as pltpu
from jax.sharding import PartitionSpec as P

VISITS = 3
NB = 128
TILE = 256
NEAR = 1
STAGES = ((0, 7),)
ROWS = 128
F32 = jnp.float32
BF16 = jnp.bfloat16
MESH = pl.DeviceIdType.MESH


def panels(count):
    wide_count = count // 2
    order = [n for n in range(wide_count)]
    return [[order[-1], order[0]], order[1:-1][::-1]]


def upper_blocks(count):
    return [
        (i, c) for half in panels(count) for panel in half for c in (2 * panel, 2 * panel + 1) for i in range(c + 1)
    ]


def wide(x):
    return jnp.broadcast_to(x, (8, NB))


def split2(x):
    hi = x.astype(BF16)
    return hi, (x - hi.astype(F32)).astype(BF16)


def split3(x):
    hi = x.astype(BF16)
    rest = x - hi.astype(F32)
    mid = rest.astype(BF16)
    return hi, mid, (rest - mid.astype(F32)).astype(BF16)


def dot(a, b):
    return jnp.dot(a, b, preferred_element_type=F32)


def dot3(a, b):
    ah, al = a
    bh, bl = b
    return dot(jnp.concatenate([ah, al], axis=1), jnp.concatenate([bh, bh], axis=0)) + dot(ah, bl)


PAIRS = ((0, 0), (0, 1), (1, 0), (1, 1), (0, 2), (2, 0))


def dot6(a, b):
    left = jnp.concatenate([a[p] for p, _ in PAIRS], axis=1)
    return dot(left, jnp.concatenate([b[q] for _, q in PAIRS], axis=0))


def outer6(a, b):
    a, b = split3(a), split3(b)
    left = jnp.concatenate([a[p] for p, _ in PAIRS], axis=0)
    right = jnp.concatenate([b[q] for _, q in PAIRS], axis=0)
    return lax.dot_general(left, right, (((0,), (0,)), ((), ())), preferred_element_type=F32)


def total(terms):
    while len(terms) > 1:
        terms = [terms[i] + terms[i + 1] for i in range(0, len(terms), 2)]
    return terms[0]


def pivot_rows(rows, k, buf):
    lane = lax.broadcasted_iota(jnp.int32, (8, NB), 1)
    sub = lax.broadcasted_iota(jnp.int32, (8, NB), 0)
    y = jnp.where((lane >= k) & (lane < k + 8), -(lane == sub + k).astype(F32), rows)
    for j in range(8):
        buf[j] = wide(rows[:, k + j : k + j + 1])
    m = [buf[j] for j in range(8)]
    for b in range(0, 8, 2):
        if b == 0:
            row = lambda i, j: wide(buf[j, i : i + 1, :])
        else:
            row = lambda i, j: wide(m[j][i : i + 1, :])
        e, f, g = row(b, b), row(b, b + 1), row(b + 1, b + 1)
        inv = 1.0 / (e * g - f * f)
        ie, jf, ig = g * inv, f * inv, e * inv
        left0 = jnp.where(sub == b, -1.0, jnp.where(sub == b + 1, 0.0, m[b]))
        left1 = jnp.where(sub == b + 1, -1.0, jnp.where(sub == b, 0.0, m[b + 1]))
        pair = (sub == b) | (sub == b + 1)

        def step(x, x0, x1):
            u0, u1 = ie * x0 - jf * x1, ig * x1 - jf * x0
            return jnp.where(pair, 0.0, x) - (left0 * u0 + left1 * u1)

        for j in range(b + 2, 8):
            m[j] = step(m[j], row(b, j), row(b + 1, j))
        y = step(y, wide(y[b : b + 1, :]), wide(y[b + 1 : b + 2, :]))
    return y


def neg_inverse(a, buf, beside=()):
    lane = lax.broadcasted_iota(jnp.int32, (8, NB), 1)
    a = list(a)
    count = len(a)
    for g in range(count):
        k = 8 * g
        own = (lane >= k) & (lane < k + 8)
        rows = a[g]
        y = pivot_rows(rows, k, buf.at[g % 2])
        near = range(g + 1, min(g + 1 + NEAR, count))
        for n in near:
            terms = [wide(a[n][:, k + j : k + j + 1]) * wide(y[j : j + 1, :]) for j in range(8)]
            a[n] = jnp.where(own, 0.0, a[n]) - total(terms)
        for call in beside[g * len(beside) // count : (g + 1) * len(beside) // count]:
            call()
        change = outer6(rows, y)
        for t in range(count):
            if t != g and t not in near:
                a[t] = jnp.where(own, 0.0, a[t]) - change[8 * t : 8 * t + 8, :]
        a[g] = y
    return a


def inverse(block, buf, beside=()):
    block = 0.5 * (block + block.T)
    tiles = [block[8 * t : 8 * t + 8, :] for t in range(NB // 8)]
    return -jnp.concatenate(neg_inverse(tiles, buf, beside), axis=0)


def solve_kernel(
    rows_total, gram_ref, right_ref, train_ref, out_ref, mat, left, right, panel, pivot, buf, held, scored, x_ref, in_sem, out_sem
):
    width = right_ref.shape[1]
    nblk = width // NB
    nrhs = right_ref.shape[0]
    rows = train_ref.shape[0]
    pieces = 2
    depth = rows // pieces
    load = pltpu.make_async_copy(train_ref, held, in_sem)
    load.start()

    eye = (lax.broadcasted_iota(jnp.int32, (NB, NB), 0) == lax.broadcasted_iota(jnp.int32, (NB, NB), 1)).astype(F32)
    blocks = upper_blocks(nblk)
    diag = jnp.zeros((NB, NB), F32)
    for n, (i, c) in enumerate(blocks):
        if i == c:
            diag = diag + gram_ref[n * NB : (n + 1) * NB, :] * eye
    trace = jnp.sum(jnp.sum(diag, axis=0, keepdims=True), axis=1, keepdims=True)
    damping = (0.1 * trace) / (rows_total * width)
    first = gram_ref[blocks.index((0, 0)) * NB : (blocks.index((0, 0)) + 1) * NB, :] * (1.0 / rows_total) + damping * eye

    def fill(n, i, c):
        def call():
            block = gram_ref[n * NB : (n + 1) * NB, :] * (1.0 / rows_total)
            if i == c:
                mat[i * NB : (i + 1) * NB, i * NB : (i + 1) * NB] = block + damping * eye
            else:
                mat[i * NB : (i + 1) * NB, c * NB : (c + 1) * NB] = block
                mat[c * NB : (c + 1) * NB, i * NB : (i + 1) * NB] = block.T

        return call

    def fill_right(c):
        def call():
            mat[:, width + c * NB : width + (c + 1) * NB] = right_ref[c * NB : (c + 1) * NB, :].astype(F32).T

        return call

    fills = [fill(n, i, c) for n, (i, c) in enumerate(blocks)] + [fill_right(c) for c in range(nrhs // NB)]

    def rows_of(j):
        return pl.ds(j * NB if isinstance(j, int) else pl.multiple_of(j * NB, NB), NB)

    def pivot_row(here, inv, c):
        def call():
            cols = slice(c, min(c + TILE, width + nrhs))
            row = split3(mat[here, cols])
            w = dot(inv, jnp.concatenate([row[q] for _, q in PAIRS], axis=0))
            wh, wl = split2(w)
            for n, part in enumerate((wh, wh, wl)):
                right[n * NB : (n + 1) * NB, cols] = part
            panel[:, cols] = w

        return call

    def pivot_column(here, some):
        hi, lo = split2(mat[some, here])
        left[some, :NB] = hi
        left[some, NB : 2 * NB] = lo
        left[some, 2 * NB :] = hi

    def update(r, c):
        def call():
            some, cols = slice(r, r + ROWS), slice(c, min(c + TILE, width + nrhs))
            mat[some, cols] -= dot(left[some, :], right[:, cols])

        return call

    def stacked_inverse():
        inv = split3(pivot[...])
        return jnp.concatenate([inv[p] for p, _ in PAIRS], axis=1)

    def step(start, j, _):
        here, there = rows_of(j), rows_of(j + 1)
        inv = stacked_inverse()
        w = dot(inv, jnp.concatenate([split3(mat[here, there])[q] for _, q in PAIRS], axis=0))
        wh, wl = split2(w)
        hi, lo = split2(mat[there, here])
        ahead = mat[there, there] - dot(
            jnp.concatenate([hi, lo, hi], axis=1), jnp.concatenate([wh, wh, wl], axis=0)
        )
        pivot_column(here, slice(0, width))
        calls = []
        for c in range(start, width + nrhs, TILE):
            pivot_row(here, inv, c)()
            calls += [update(r, c) for r in range(0, width, ROWS)]
        pivot[...] = inverse(ahead, buf, calls)
        mat[here, start:] = panel[:, start:]
        return 0

    pivot[...] = inverse(first, buf, fills)
    for first, last in STAGES:
        lax.fori_loop(first, last, functools.partial(step, (first + 1) * NB), 0)
    here = rows_of(nblk - 1)
    pivot_column(here, slice(0, width))
    for c in range(width, width + nrhs, TILE):
        pivot_row(here, stacked_inverse(), c)()
        for r in range(0, width, ROWS):
            update(r, c)()
    mat[here, width:] = panel[:, width:]
    x_ref[...] = mat[:, width:].astype(BF16)
    load.wait()
    scale = 1.0 / (width ** 0.5)

    def score(p, _):
        part = pl.ds(pl.multiple_of(p * depth, depth), depth)
        scored[part, :] = (dot(held[part, :], x_ref[...]) * scale).astype(BF16)
        pltpu.make_async_copy(scored.at[part], out_ref.at[part], out_sem).start()
        return 0

    lax.fori_loop(0, pieces, score, 0)
    pltpu.make_async_copy(scored, out_ref, out_sem).wait()


def solve_and_score(gram, right, train, rows_total):
    rows, width = train.shape
    nrhs = right.shape[0]
    return pl.pallas_call(
        functools.partial(solve_kernel, rows_total),
        out_shape=jax.ShapeDtypeStruct((rows, nrhs), BF16),
        in_specs=[
            pl.BlockSpec(memory_space=pltpu.VMEM),
            pl.BlockSpec(memory_space=pltpu.VMEM),
            pl.BlockSpec(memory_space=pl.ANY),
        ],
        out_specs=pl.BlockSpec(memory_space=pl.ANY),
        scratch_shapes=[
            pltpu.VMEM((width, width + nrhs), F32),
            pltpu.VMEM((width, 3 * NB), BF16),
            pltpu.VMEM((3 * NB, width + nrhs), BF16),
            pltpu.VMEM((NB, width + nrhs), F32),
            pltpu.VMEM((NB, NB), F32),
            pltpu.VMEM((2, 8, 8, NB), F32),
            pltpu.VMEM((rows, width), BF16),
            pltpu.VMEM((rows, nrhs), BF16),
            pltpu.VMEM((width, nrhs), BF16),
            pltpu.SemaphoreType.DMA,
            pltpu.SemaphoreType.DMA,
        ],
        compiler_params=pltpu.CompilerParams(vmem_limit_bytes=56 << 20),
        name="solve_and_score",
    )(gram, right, train)


RING = 4
PARTS = 3


def gram_panel(panel, known, held, turned, gram, loads, place):
    rows = held.shape[0]
    depth = rows // len(loads)
    last = (panel + 1) * 2 * NB
    for k, load in enumerate(loads):
        if load is not None:
            load.wait()
        some = slice(k * depth, (k + 1) * depth)
        if known < last:
            turned[known:last, some] = held[some, known:last].T
        res = dot(turned[:last, some], held[some, panel * 2 * NB : last])
        for n in range(2):
            c = 2 * panel + n
            for i in range(c + 1):
                spot = slice(place[i, c] * NB, place[i, c] * NB + NB)
                block = res[i * NB : (i + 1) * NB, n * NB : (n + 1) * NB]
                if k == 0:
                    gram[spot, :] = block
                else:
                    gram[spot, :] += block
    return max(known, last)


def sum_kernel(
    train_ref, target_ref, out_ref, right_ref, held, turned, gram_ref, pair, work, got1, sum1, got2, sum2, got3, full2,
    send0, recv0, send1, recv1, send2, recv2, send3, recv3, send4, recv4, send5, recv5, send6, recv6, send7, recv7,
    own_sem, load_sem,
):
    chunks = load_sem.shape[0]
    depth = held.shape[0] // chunks
    loads = [
        pltpu.make_async_copy(train_ref.at[pl.ds(k * depth, depth)], held.at[pl.ds(k * depth, depth)], load_sem.at[k])
        for k in range(chunks)
    ]
    for load in loads:
        load.start()
    nblk = held.shape[1] // NB
    halves = panels(nblk)
    place = {key: n for n, key in enumerate(upper_blocks(nblk))}
    grp, blk = lax.axis_index("grp"), lax.axis_index("blk")
    core = lax.rem(grp, 2)
    pos = (lax.rem(blk, 2) * 2 + grp // 2, blk // 8, lax.rem(blk // 2, RING))

    def device(where, which):
        x, y, z = where
        return (lax.rem(x, 2) * 2 + which, (y * RING + z) * 2 + x // 2)

    def along(axis, d):
        where = list(pos)
        where[axis] = lax.rem(where[axis] + d, RING)
        return device(where, core)

    mate = device(pos, 1 - core)
    blks = lax.axis_size("blk")
    ahead = [(grp, lax.rem(blk + s, blks)) for s in range(1, VISITS)]
    behind = [(grp, lax.rem(blk + blks - s, blks)) for s in range(1, VISITS)]
    mates = [mate] + [along(axis, d) for axis in range(3) for d in range(1, RING)]

    barrier = pltpu.get_barrier_semaphore()
    for other in mates + behind:
        pl.semaphore_signal(barrier, inc=1, device_id=other, device_id_type=MESH)

    done = [None] * chunks
    for c in range(2):

        @pl.when(core == c)
        def _():
            known = 0
            for n, panel in enumerate(halves[1 - c]):
                known = gram_panel(panel, known, held, turned, gram_ref, done if n else loads, place)

    pl.semaphore_wait(barrier, len(mates) + len(ahead))

    def remote(src, dst, send, recv, who):
        return pltpu.make_async_remote_copy(
            src_ref=src, dst_ref=dst, send_sem=send, recv_sem=recv, device_id=who, device_id_type=MESH
        )

    half = gram_ref.shape[0] // 2
    third = half // PARTS
    q1 = third // RING
    q2 = q1 // RING

    def rows(start, size):
        return pl.ds(pl.multiple_of(start, 8), size)

    c0, c1, c2, c3, c4, c5, c6, c7 = {}, {}, {}, {}, {}, {}, {}, {}
    for p in range(PARTS):
        c0[p] = remote(
            gram_ref.at[rows((1 - core) * half + p * third, third)], pair.at[p], send0.at[p], recv0.at[p], mate
        )
        c0[p].start()
    nt = target_ref.shape[0]
    for s in range(1, VISITS):
        c7[s] = remote(target_ref, right_ref.at[pl.ds(s * nt, nt)], send7.at[s - 1], recv7.at[s - 1], ahead[s - 1])
        c7[s].start()
    own = [pltpu.make_async_copy(target_ref, right_ref.at[pl.ds(0, nt)], own_sem.at[PARTS])]
    own[0].start()
    for c in range(2):

        @pl.when(core == c)
        def _():
            known = 2 * NB * (max(halves[1 - c]) + 1)
            for panel in halves[c]:
                known = gram_panel(panel, known, held, turned, gram_ref, done, place)

    steps = range(1, RING)
    for p in range(PARTS):
        axis = p
        c0[p].wait_recv()
        work[p] = gram_ref[rows(core * half + p * third, third), :] + pair[p]
        for d in steps:
            c1[p, d] = remote(
                work.at[p, rows(lax.rem(pos[axis] + d, RING) * q1, q1)],
                got1.at[p, d - 1], send1.at[p, d - 1], recv1.at[p, d - 1], along(axis, d),
            )
            c1[p, d].start()
    for p in range(PARTS):
        axis = (p + 1) % 3
        for d in steps:
            c1[p, d].wait_recv()
        mine = work[p, rows(pos[p] * q1, q1), :]
        sum1[p] = (mine + got1[p, 0]) + (got1[p, 1] + got1[p, 2])
        for d in steps:
            c2[p, d] = remote(
                sum1.at[p, rows(lax.rem(pos[axis] + d, RING) * q2, q2)],
                got2.at[p, d - 1], send2.at[p, d - 1], recv2.at[p, d - 1], along(axis, d),
            )
            c2[p, d].start()
    for p in range(PARTS):
        axis = (p + 2) % 3
        for d in steps:
            c2[p, d].wait_recv()
        mine = sum1[p, rows(pos[(p + 1) % 3] * q2, q2), :]
        sum2[p] = (mine + got2[p, 0]) + (got2[p, 1] + got2[p, 2])
        for d in steps:
            c3[p, d] = remote(sum2.at[p], got3.at[p, d - 1], send3.at[p, d - 1], recv3.at[p, d - 1], along(axis, d))
            c3[p, d].start()
    for p in range(PARTS):
        axis = (p + 1) % 3
        for d in steps:
            c3[p, d].wait_recv()
        spot = rows(pos[axis] * q2, q2)
        full2[p, spot, :] = (sum2[p] + got3[p, 0]) + (got3[p, 1] + got3[p, 2])
        for d in steps:
            c4[p, d] = remote(
                full2.at[p, spot], full2.at[p, spot], send4.at[p, d - 1], recv4.at[p, d - 1], along(axis, d)
            )
            c4[p, d].start()
    for p in range(PARTS):
        for d in steps:
            c4[p, d].wait_recv()
        spot = rows(core * half + p * third + pos[p] * q1, q1)
        for d in steps:
            c5[p, d] = remote(full2.at[p], out_ref.at[spot], send5.at[p, d - 1], recv5.at[p, d - 1], along(p, d))
            c5[p, d].start()
        c6[p, 0] = remote(full2.at[p], out_ref.at[spot], send6.at[p, 0], recv6.at[p, 0], mate)
        c6[p, 0].start()
        own.append(pltpu.make_async_copy(full2.at[p], out_ref.at[spot], own_sem.at[p]))
        own[-1].start()
    for d in (1, 3, 2):
        for p in range(PARTS):
            c5[p, d].wait_recv()
            spot = rows(core * half + p * third + lax.rem(pos[p] + RING - d, RING) * q1, q1)
            c6[p, d] = remote(out_ref.at[spot], out_ref.at[spot], send6.at[p, d], recv6.at[p, d], mate)
            c6[p, d].start()
    for copies in (c0, c1, c2, c3, c4, c5, c6, c7):
        for copy in copies.values():
            copy.wait_send()
    for copy in own:
        copy.wait()
    for copies in (c6, c7):
        for copy in copies.values():
            copy.wait_recv()


def summed_gram(train, targets):
    rows, width = train.shape
    total_rows = len(upper_blocks(width // NB)) * NB
    third = total_rows // (2 * PARTS)
    q1, q2 = third // RING, third // (RING * RING)
    sem = pltpu.SemaphoreType.DMA
    fan = RING - 1
    pairs = [(PARTS,)] + [(PARTS, fan)] * 5 + [(PARTS, RING), (VISITS - 1,)]
    return pl.pallas_call(
        sum_kernel,
        out_shape=(
            jax.ShapeDtypeStruct((total_rows, NB), F32),
            jax.ShapeDtypeStruct((VISITS * targets.shape[0], targets.shape[1]), BF16),
        ),
        in_specs=[pl.BlockSpec(memory_space=pl.ANY)] * 2,
        out_specs=[pl.BlockSpec(memory_space=pl.ANY)] * 2,
        scratch_shapes=[
            pltpu.VMEM((rows, width), BF16),
            pltpu.VMEM((width, rows), BF16),
            pltpu.VMEM((total_rows, NB), F32),
            pltpu.VMEM((PARTS, third, NB), F32),
            pltpu.VMEM((PARTS, third, NB), F32),
            pltpu.VMEM((PARTS, fan, q1, NB), F32),
            pltpu.VMEM((PARTS, q1, NB), F32),
            pltpu.VMEM((PARTS, fan, q2, NB), F32),
            pltpu.VMEM((PARTS, q2, NB), F32),
            pltpu.VMEM((PARTS, fan, q2, NB), F32),
            pltpu.VMEM((PARTS, q1, NB), F32),
        ]
        + [sem(shape) for shape in pairs for _ in range(2)]
        + [sem((PARTS + 1,)), sem((4,))],
        compiler_params=pltpu.CompilerParams(
            collective_id=0, has_side_effects=True, vmem_limit_bytes=56 << 20
        ),
        name="summed_gram",
    )(train, targets)


def per_device(train_grads, targets):
    rows_total = train_grads.shape[0] * lax.axis_size("grp") * lax.axis_size("blk")
    gram, right = summed_gram(train_grads, targets)
    return solve_and_score(gram, right, train_grads, rows_total)


def solution(mesh):
    spec = P(("grp", "blk"), None)
    return jax.shard_map(per_device, mesh=mesh, in_specs=(spec, spec), out_specs=spec, check_vma=False)
```
